32 devices in a mesh: groups: 2 (over y), cuts: 4 (over z), rep: 2 (over x), sub: 2 (over core).
Axes of the slice: x: 2, y: 2, z: 4, core: 2. Of those that a mesh axis runs over, the one named last changes fastest.
Arguments:
- features: bfloat16 [4096, 4096], P(('groups', 'rep', 'sub'), 'cuts'), parts along dimension 0, may hold values from -6 to 6
- w_self1: bfloat16 [4096, 512], P('cuts'), may hold values from -0.09375 to 0.09375
- w_neigh1: bfloat16 [4096, 512], P('cuts'), may hold values from -0.09375 to 0.09375
- bias1: float32 [512], replicated, may hold values from -3 to 3
- w_self2: bfloat16 [512, 512], replicated, may hold values from -0.25 to 0.25
- w_neigh2: bfloat16 [512, 512], replicated, may hold values from -0.25 to 0.25
- bias2: float32 [512], replicated, may hold values from -3 to 3
- degree: int32 [8, 512], P(('groups', 'rep', 'sub')), parts along dimension 0, may hold values from 16 to 159
- neighbor_owners: int32 [8, 4, 3], P(('groups', 'rep', 'sub')), parts along dimension 0, may hold values from 0 to 3, as said below
- neighbor_count: int32 [8, 4], P(('groups', 'rep', 'sub')), parts along dimension 0, may hold values from 1 to 3, as said below
- boundary_rows: int32 [8, 4, 3, 32], P(('groups', 'rep', 'sub')), parts along dimension 0, may hold values from 0 to 127, as said below
- boundary_count: int32 [8, 4, 3], P(('groups', 'rep', 'sub')), parts along dimension 0, may hold values from 16 to 32, as said below
- edge_weight: bfloat16 [8, 4, 3, 32, 128], P(('groups', 'rep', 'sub')), parts along dimension 0, may hold values from 0.5 to 1.5
- node_id: int32 [8, 512], P(('groups', 'rep', 'sub'), 'cuts'), parts along dimension 0, may hold values from 0 to 2047, as said below
Outputs:
- embeddings: bfloat16 [4096, 512], P(('groups', 'cuts', 'rep', 'sub')), parts along dimension 0
The draws below stay inside these ranges and needn't reach their ends.
There are 2 independent parts, one for each index of `groups`. The reference program is written for one: setup_inputs(seed, part) draws one part's arguments, and reference() takes and returns one part's arrays. A program takes and returns all parts, laid end to end along the dimension named above; an argument that names none is the same for every part. Nothing has to cross between parts.
Inputs may be any that keep to these rules, and one draw needn't show every extreme that they name: `neighbor_owners`: each list holds 3 distinct owners. `neighbor_count`: every block has an owner whose count is 3. `boundary_rows`: distinct within each list. `boundary_count`: every block has a list whose count is 32. `node_id`: A permutation. Call block b's nodes u * 128 to (u + 1) * 128 - 1 owner (b,u) and ids d * 128 to (d + 1) * 128 - 1 range d; owner (b,u) holds exactly 16 id of each range d with d mod 2 = b mod 2, and none of others.
All inputs are finite; a program needn't handle non-finite values.
Results may differ from the reference program's by a relative error of at most 0.0045.
Values may be sent and summed in bfloat16 or wider, within the bound.
No kernel may reach another device: no remote copies, remote signals or barrier semaphores. Data moves between devices by JAX's collectives and lax.ppermute only.
A program may use at most 64 MiB of HBM per device.

```python
import jax
import jax.numpy as jnp
from jax import lax

F = 4096
H = 512
ROWS_DEV = 128
BCAP = 32
NEIGH = 3
SLAB_ROWS = 512
BLOCKS = 4
NODES = 2048
PEER_ROWS = 16
N_CUTS = 4
N_REP = 2
N_SUB = 2


def distinct_order(key, shape, length):
    top = (2 ** 31 - 1) // length
    scores = jax.random.randint(key, shape + (length,), 0, top) * length
    scores = scores + jnp.arange(length, dtype=jnp.int32)
    return jnp.argsort(scores, axis=-1).astype(jnp.int32)


def draw_neighbor_owners(key, part):
    key = jax.random.fold_in(key, 11)
    order_all = distinct_order(key, (BLOCKS, N_CUTS), N_CUTS)
    return order_all[:, :, :NEIGH]


def draw_neighbor_count(key, part):
    key = jax.random.fold_in(key, 12)
    first_key, second_key = jax.random.split(key)
    lowest = max(NEIGH // 2, 1)
    values = jax.random.randint(first_key, (BLOCKS, N_CUTS), lowest, NEIGH + 1)
    chosen = jax.random.randint(second_key, (BLOCKS, 1), 0, N_CUTS)
    slots = jnp.arange(N_CUTS, dtype=jnp.int32)[None, :]
    return jnp.where(slots == chosen, NEIGH, values).astype(jnp.int32)


def draw_boundary_rows(key, part):
    key = jax.random.fold_in(key, 13)
    order_all = distinct_order(key, (BLOCKS, N_CUTS, NEIGH), ROWS_DEV)
    return order_all[:, :, :, :BCAP]


def draw_boundary_count(key, part):
    key = jax.random.fold_in(key, 14)
    first_key, second_key = jax.random.split(key)
    lowest = max(BCAP // 2, 1)
    values = jax.random.randint(first_key, (BLOCKS, N_CUTS * NEIGH), lowest, BCAP + 1)
    chosen = jax.random.randint(second_key, (BLOCKS, 1), 0, N_CUTS * NEIGH)
    slots = jnp.arange(N_CUTS * NEIGH, dtype=jnp.int32)[None, :]
    values = jnp.where(slots == chosen, BCAP, values)
    return values.reshape(BLOCKS, N_CUTS, NEIGH).astype(jnp.int32)


def draw_node_id(key, part):
    key = jax.random.fold_in(key, 15)
    first_key, second_key = jax.random.split(key)
    slot_of = distinct_order(first_key, (N_REP, N_SUB, N_CUTS), ROWS_DEV)
    peer_dest = slot_of // PEER_ROWS
    offset = slot_of % PEER_ROWS
    rep_pos = jnp.arange(N_REP, dtype=jnp.int32)[:, None, None, None]
    sub_pos = jnp.arange(N_SUB, dtype=jnp.int32)[None, :, None, None]
    cut_pos = jnp.arange(N_CUTS, dtype=jnp.int32)[None, None, :, None]
    source_peer = cut_pos * N_REP + rep_pos
    arrival = source_peer * PEER_ROWS + offset
    dest_device = peer_dest // N_REP * (N_REP * N_SUB) + peer_dest % N_REP * N_SUB + sub_pos
    shuffle = distinct_order(second_key, (BLOCKS * N_CUTS,), ROWS_DEV)
    ids_all = dest_device * ROWS_DEV + shuffle[dest_device, arrival]
    return ids_all.reshape(BLOCKS, SLAB_ROWS).astype(jnp.int32)


def with_ends(entries, key, low, top_value):
    spot = [jax.random.randint(jax.random.fold_in(key, axis), (), 0, length) for axis, length in enumerate(entries.shape)]
    longest = entries.shape.index(max(entries.shape))
    next_to = spot[:longest] + [(spot[longest] + 1) % entries.shape[longest]] + spot[longest + 1:]
    return entries.at[tuple(spot)].set(low).at[tuple(next_to)].set(top_value)


def levels(rng, dims, cuts, low, top_value):
    level = 1.0
    for axis_at, shards_of in cuts:
        steps = jax.random.uniform(jax.random.fold_in(jax.random.fold_in(rng, 6), axis_at), (shards_of,), jnp.float32, low / len(cuts), top_value / len(cuts))
        level = level * jnp.repeat(jnp.exp(steps), dims[axis_at] // shards_of).reshape((-1,) + (1,) * (len(dims) - 1 - axis_at))
    return level


def gaussian(key, extent, deviation, most, cuts=(), kind=jnp.bfloat16):
    gain = levels(key, extent, cuts, -0.22, 0.18) if cuts else 1.0
    result = jax.random.normal(key, extent, jnp.float32) * deviation * gain
    return jnp.minimum(jnp.maximum(result, -most), most).astype(kind)


def setup_inputs(seed: int = 0, part: int = 0) -> dict:
    splits = jax.random.split(jax.random.key(seed), 15)
    part_keys = jax.random.split(jax.random.fold_in(splits[14], part), 15)
    return {
        "features": gaussian(part_keys[0], (NODES, F), 1.0, 6.0, ((0, 4), (1, 4))),
        "w_self1": gaussian(splits[1], (F, H), F ** -0.5, 0.09375, ((0, 4),)),
        "w_neigh1": gaussian(splits[2], (F, H), F ** -0.5, 0.09375, ((0, 4),)),
        "bias1": gaussian(splits[3], (H,), 0.5, 3.0, (), jnp.float32),
        "w_self2": gaussian(splits[4], (H, H), H ** -0.5, 0.25),
        "w_neigh2": gaussian(splits[5], (H, H), H ** -0.5, 0.25),
        "bias2": gaussian(splits[6], (H,), 0.5, 3.0, (), jnp.float32),
        "degree": with_ends(jax.random.randint(part_keys[7], (BLOCKS, SLAB_ROWS), 16, 160), jax.random.fold_in(part_keys[7], 1), 16, 159).astype(jnp.int32),
        "neighbor_owners": draw_neighbor_owners(jax.random.fold_in(jax.random.fold_in(splits[14], part), 71), part),
        "neighbor_count": draw_neighbor_count(jax.random.fold_in(jax.random.fold_in(splits[14], part), 71), part),
        "boundary_rows": draw_boundary_rows(jax.random.fold_in(jax.random.fold_in(splits[14], part), 71), part),
        "boundary_count": draw_boundary_count(jax.random.fold_in(jax.random.fold_in(splits[14], part), 71), part),
        "edge_weight": jnp.clip(0.5 + 1.0 * jax.random.uniform(part_keys[12], (BLOCKS, N_CUTS, NEIGH, BCAP, ROWS_DEV), jnp.float32) ** levels(part_keys[12], (BLOCKS, N_CUTS, NEIGH, BCAP, ROWS_DEV), ((0, 4),), -0.2, 0.2), 0.5, 1.5).astype(jnp.bfloat16),
        "node_id": draw_node_id(jax.random.fold_in(jax.random.fold_in(splits[14], part), 71), part),
    }


def aggregate(source_rows, owner_lists, owner_counts, row_lists, row_counts, edge_weights, degrees_block):
    picked = source_rows[owner_lists[:, :, None], row_lists].astype(jnp.float32)
    owner_mask = jnp.arange(NEIGH)[None, :] < owner_counts[:, None]
    slot_mask = jnp.arange(BCAP)[None, None, :] < row_counts[:, :, None]
    full_mask = (owner_mask[:, :, None] & slot_mask).astype(jnp.float32)
    live_weight = edge_weights.astype(jnp.float32) * full_mask[:, :, :, None]
    summed = jnp.einsum('uksi,uksw->uiw', live_weight, picked, precision=lax.Precision.HIGHEST)
    summed = summed.reshape(SLAB_ROWS, source_rows.shape[2])
    return summed / degrees_block[:, None].astype(jnp.float32)

def reference(features, w_self1, w_neigh1, bias1, w_self2, w_neigh2, bias2, degree, neighbor_owners, neighbor_count, boundary_rows, boundary_count, edge_weight, node_id):
    feature_table = features.reshape(BLOCKS, N_CUTS, ROWS_DEV, F)
    neigh_full = w_neigh1.astype(jnp.float32)

    def first_layer(block_args):
        block_rows, owner_lists, owner_counts, row_lists, row_counts, edge_weights, degrees_block = block_args
        agg_one = aggregate(block_rows, owner_lists, owner_counts, row_lists, row_counts, edge_weights, degrees_block)
        flat_rows = block_rows.reshape(SLAB_ROWS, F)
        pre_act = jnp.dot(flat_rows, w_self1, preferred_element_type=jnp.float32)
        pre_act = pre_act + jnp.dot(agg_one, neigh_full, precision=lax.Precision.HIGHEST) + bias1
        return jnp.maximum(pre_act, 0.0).astype(jnp.bfloat16).reshape(N_CUTS, ROWS_DEV, H)
    layer_one = lax.map(first_layer, (feature_table, neighbor_owners, neighbor_count, boundary_rows, boundary_count, edge_weight, degree))

    def second_layer(block_args):
        block_rows, owner_lists, owner_counts, row_lists, row_counts, edge_weights, degrees_block = block_args
        agg_two = aggregate(block_rows, owner_lists, owner_counts, row_lists, row_counts, edge_weights, degrees_block).astype(jnp.bfloat16)
        flat_rows = block_rows.reshape(SLAB_ROWS, H)
        z_value = jnp.dot(flat_rows, w_self2, preferred_element_type=jnp.float32)
        z_value = z_value + jnp.dot(agg_two, w_neigh2, preferred_element_type=jnp.float32) + bias2
        scale = lax.rsqrt(lax.optimization_barrier(jnp.mean(z_value * z_value, axis=1, keepdims=True)) + 1e-05)
        return (z_value * scale).astype(jnp.bfloat16)
    normalized = lax.map(second_layer, (layer_one, neighbor_owners, neighbor_count, boundary_rows, boundary_count, edge_weight, degree))
    normalized = normalized.reshape(NODES, H)
    embeddings = jnp.zeros((NODES, H), jnp.bfloat16)
    return embeddings.at[node_id.reshape(NODES)].set(normalized)
```

```python
import functools

import jax
import jax.numpy as jnp
from jax import lax
from jax.experimental import pallas as pl
from jax.experimental.pallas import tpu as pltpu
from jax.sharding import PartitionSpec as P

F32 = jnp.float32
BF16 = jnp.bfloat16
VMEM = pltpu.VMEM
SMEM = pltpu.SMEM


def partner(index, step, total):
    if total & (total - 1) == 0:
        return index ^ step
    return lax.rem(step - index + 2 * total, total)


def partner_pairs(step, total):
    if total & (total - 1) == 0:
        return [(i, i ^ step) for i in range(total)]
    return [(i, (step - i) % total) for i in range(total)]


def as_column(row):
    n = row.shape[1]
    eye = lax.broadcasted_iota(jnp.int32, (n, n), 0) == lax.broadcasted_iota(jnp.int32, (n, n), 1)
    return jnp.sum(jnp.where(eye, jnp.broadcast_to(row, (n, n)), 0.0), axis=1, keepdims=True)


def live_limit(count_ref, bcount_ref, owner, k):
    return jnp.where(k < count_ref[0, owner], bcount_ref[0, owner, k], 0)


def live_tile(ew_ref, count_ref, bcount_ref, owner):
    _, _, neigh, cap, rows = ew_ref.shape
    slot = lax.broadcasted_iota(jnp.int32, (cap, rows), 0)
    tiles = []
    for k in range(neigh):
        live = slot < live_limit(count_ref, bcount_ref, owner, k)
        tiles.append(jnp.where(live, ew_ref[0, owner, k].astype(F32), 0.0).astype(BF16))
    return jnp.concatenate(tiles, axis=0)


def contract_first(a, b):
    return lax.dot_general(a, b, (((0,), (0,)), ((), ())), preferred_element_type=F32)


def contract_last(a, b):
    return lax.dot_general(a, b, (((1,), (1,)), ((), ())), preferred_element_type=F32)


def first_layer_kernel(
    cuts, owners_ref, count_ref, bcount_ref, x_hbm, wn_hbm, ws_hbm, deg_ref, brow_ref, ew_ref, *rest
):
    outs = rest[:cuts]
    x_v, wn_v, ws_v, pick_v, y_v, s_v, sb_v, sems = rest[cuts:]
    copies = [
        pltpu.make_async_copy(src, dst, sems.at[i])
        for i, (src, dst) in enumerate(((x_hbm, x_v), (wn_hbm, wn_v), (ws_hbm, ws_v)))
    ]
    for copy in copies:
        copy.start()
    _, _, neigh, cap, rows = ew_ref.shape
    total = cuts * rows
    me = lax.axis_index("cuts")
    lane = lax.broadcasted_iota(jnp.int32, (cap, total), 1)
    eye = (
        lax.broadcasted_iota(jnp.int32, (cap, cap), 0) == lax.broadcasted_iota(jnp.int32, (cap, cap), 1)
    ).astype(F32)
    for u in range(cuts):
        columns = contract_last(eye, brow_ref[0, u].astype(F32)).astype(jnp.int32)
        for k in range(neigh):
            target = columns[:, k : k + 1] + owners_ref[0, u, k] * rows
            pick_v[u, k * cap : (k + 1) * cap, :] = (lane == target).astype(F32).astype(BF16)
    copies[0].wait()
    copies[1].wait()
    y_v[...] = jnp.dot(x_v[...], wn_v[...], preferred_element_type=F32).astype(BF16)
    copies[2].wait()
    s_v[...] = jnp.dot(x_v[...], ws_v[...], preferred_element_type=F32)
    for u in range(cuts):
        at = slice(u * rows, (u + 1) * rows)
        picked = jnp.dot(pick_v[u], y_v[...], preferred_element_type=F32).astype(BF16)
        summed = contract_first(live_tile(ew_ref, count_ref, bcount_ref, u), picked)
        scale = as_column(1.0 / deg_ref[:, at].astype(F32))
        sb_v[at, :] = (s_v[at, :] + summed * scale).astype(BF16)
    for step in range(cuts):
        u = partner(me, step, cuts)
        outs[step][:rows, :] = sb_v[pl.ds(pl.multiple_of(u * rows, rows), rows), :]
        outs[step][rows:, :] = jnp.dot(pick_v[u], sb_v[...], preferred_element_type=F32).astype(BF16)


def second_layer_kernel(cuts, reps, subs, count_ref, bcount_ref, *rest):
    slabs = rest[:cuts]
    b1_ref, ws_ref, wn_ref, b2_ref, deg_ref, ew_ref, id_ref, out_ref = rest[cuts:]
    rows = ew_ref.shape[4]
    units = ws_ref.shape[0]
    me = lax.axis_index("cuts")
    total = slabs[0][...].astype(F32)
    for slab in slabs[1:]:
        total = total + slab[...].astype(F32)
    hidden = jnp.maximum(total + b1_ref[...], 0.0).astype(BF16)
    own, border = hidden[:rows], hidden[rows:]
    summed = contract_first(live_tile(ew_ref, count_ref, bcount_ref, me), border)
    degrees = deg_ref[:, pl.ds(pl.multiple_of(me * rows, rows), rows)].astype(F32)
    mean = (summed * as_column(1.0 / degrees)).astype(BF16)
    z = jnp.dot(own, ws_ref[...], preferred_element_type=F32)
    z = z + jnp.dot(mean, wn_ref[...], preferred_element_type=F32) + b2_ref[...]
    scale = lax.rsqrt(jnp.mean(z * z, axis=1, keepdims=True) + 1e-05)
    normalized = (z * scale).astype(BF16)
    ids = id_ref[...]
    device = ids // rows
    peer = (device // (reps * subs)) * reps + (device // subs) % reps
    slot = (ids - device * rows).astype(F32)
    peer_f = peer.astype(F32)
    down = lax.broadcasted_iota(jnp.int32, (rows, rows), 0)
    across = lax.broadcasted_iota(jnp.int32, (rows, rows), 1)
    earlier = (as_column(peer_f) == peer_f) & (down < across)
    rank = jnp.sum(earlier.astype(F32), axis=0, keepdims=True).astype(jnp.int32)
    place = peer * (rows // (cuts * reps)) + rank
    chosen = down == place
    out_ref[:, :units] = jnp.dot(chosen.astype(F32).astype(BF16), normalized, preferred_element_type=F32).astype(BF16)
    slots = jnp.sum(jnp.where(chosen, slot, 0.0), axis=1, keepdims=True)
    out_ref[:, units:] = jnp.broadcast_to(slots, (rows, rows)).astype(BF16)


def placing_kernel(in_ref, out_ref):
    rows, units = out_ref.shape
    across = lax.broadcasted_iota(jnp.int32, (rows, rows), 1)
    chosen = in_ref[:, units:].astype(F32).astype(jnp.int32) == across
    out_ref[...] = contract_first(chosen.astype(F32).astype(BF16), in_ref[:, :units]).astype(BF16)


def body(
    features,
    w_self1,
    w_neigh1,
    bias1,
    w_self2,
    w_neigh2,
    bias2,
    degree,
    neighbor_owners,
    neighbor_count,
    boundary_rows,
    boundary_count,
    edge_weight,
    node_id,
):
    cuts, reps, subs = (lax.axis_size(a) for a in ("cuts", "rep", "sub"))
    total, width = features.shape
    units = w_self1.shape[1]
    _, _, neigh, cap, rows = edge_weight.shape
    border = neigh * cap
    smem = pl.BlockSpec(memory_space=SMEM)
    vmem = pl.BlockSpec(memory_space=VMEM)
    hbm = pl.BlockSpec(memory_space=pl.ANY)
    slab = jax.ShapeDtypeStruct((rows + border, units), BF16)
    held = 2 * (total * width + 2 * width * units + cuts * border * total + 4 * total * units)
    held += 2 * cuts * (rows + border) * units + 8 * total * units
    slabs = pl.pallas_call(
        functools.partial(first_layer_kernel, cuts),
        out_shape=[slab] * cuts,
        in_specs=[smem] * 3 + [hbm] * 3 + [vmem] * 3,
        out_specs=[vmem] * cuts,
        scratch_shapes=[
            pltpu.VMEM((total, width), BF16),
            pltpu.VMEM((width, units), BF16),
            pltpu.VMEM((width, units), BF16),
            pltpu.VMEM((cuts, border, total), BF16),
            pltpu.VMEM((total, units), BF16),
            pltpu.VMEM((total, units), F32),
            pltpu.VMEM((total, units), BF16),
            pltpu.SemaphoreType.DMA((3,)),
        ],
        compiler_params=pltpu.CompilerParams(vmem_limit_bytes=held + (8 << 20)),
        name="first_layer",
    )(neighbor_owners, neighbor_count, boundary_count, features, w_neigh1, w_self1, degree, boundary_rows, edge_weight)
    arrived = [slabs[0]]
    order = sorted(range(1, cuts), key=lambda s: (-(s & (s - 1)) if s > 1 else 1, s))
    got = {s: lax.ppermute(slabs[s], "cuts", partner_pairs(s, cuts)) for s in order}
    arrived += [got[s] for s in range(1, cuts)]
    payload = pl.pallas_call(
        functools.partial(second_layer_kernel, cuts, reps, subs),
        out_shape=jax.ShapeDtypeStruct((rows, units + rows), BF16),
        in_specs=[smem] * 2 + [vmem] * (cuts + 7),
        out_specs=vmem,
        compiler_params=pltpu.CompilerParams(vmem_limit_bytes=24 << 20),
        name="second_layer",
    )(
        neighbor_count,
        boundary_count,
        *arrived,
        bias1.reshape(1, units),
        w_self2,
        w_neigh2,
        bias2.reshape(1, units),
        degree,
        edge_weight,
        node_id,
    )
    peers = cuts * reps
    moved = lax.all_to_all(
        payload.reshape(peers, rows // peers, units + rows), ("cuts", "rep"), split_axis=0, concat_axis=0, tiled=True
    )
    return pl.pallas_call(
        placing_kernel,
        out_shape=jax.ShapeDtypeStruct((rows, units), BF16),
        in_specs=[vmem],
        out_specs=vmem,
        name="placing",
    )(moved.reshape(rows, units + rows))


def solution(mesh):
    block = ("groups", "rep", "sub")
    placed = (
        P(block, "cuts"),
        P("cuts", None),
        P("cuts", None),
        P(),
        P(),
        P(),
        P(),
        P(block, None),
        P(block, None, None),
        P(block, None),
        P(block, None, None, None),
        P(block, None, None),
        P(block, None, None, None, None),
        P(block, "cuts"),
    )
    return jax.shard_map(
        body,
        mesh=mesh,
        in_specs=placed,
        out_specs=P(("groups", "cuts", "rep", "sub"), None),
        check_vma=False,
    )
```

```python
import functools

import jax
import jax.numpy as jnp
from jax import lax
from jax.experimental import pallas as pl
from jax.experimental.pallas import tpu as pltpu
from jax.sharding import PartitionSpec as P

F32 = jnp.float32
BF16 = jnp.bfloat16
VMEM = pltpu.VMEM
SMEM = pltpu.SMEM


def partner(index, step, total):
    if total & (total - 1) == 0:
        return index ^ step
    return lax.rem(step - index + 2 * total, total)


def partner_pairs(step, total):
    if total & (total - 1) == 0:
        return [(i, i ^ step) for i in range(total)]
    return [(i, (step - i) % total) for i in range(total)]


def as_column(row):
    n = row.shape[1]
    eye = lax.broadcasted_iota(jnp.int32, (n, n), 0) == lax.broadcasted_iota(jnp.int32, (n, n), 1)
    return jnp.sum(jnp.where(eye, jnp.broadcast_to(row, (n, n)), 0.0), axis=1, keepdims=True)


def live_limit(count_ref, bcount_ref, owner, k):
    return jnp.where(k < count_ref[0, owner], bcount_ref[k, 0, owner], 0)


def live_tile(tile, count_ref, bcount_ref, owner):
    neigh, cap, rows = tile.shape
    slot = lax.broadcasted_iota(jnp.int32, (cap, rows), 0)
    tiles = []
    for k in range(neigh):
        live = slot < live_limit(count_ref, bcount_ref, owner, k)
        tiles.append(jnp.where(live, tile[k].astype(F32), 0.0).astype(BF16))
    return jnp.concatenate(tiles, axis=0)


def contract_first(a, b):
    return lax.dot_general(a, b, (((0,), (0,)), ((), ())), preferred_element_type=F32)


def contract_last(a, b):
    return lax.dot_general(a, b, (((1,), (1,)), ((), ())), preferred_element_type=F32)


def in_hbm(*arrays):
    return [pltpu.with_memory_space_constraint(a, pltpu.HBM) for a in arrays]


def start_all(pairs, sems):
    copies = [pltpu.make_async_copy(src, dst, sems.at[i]) for i, (src, dst) in enumerate(pairs)]
    for copy in copies:
        copy.start()
    return copies


def fill_slab(out_ref, sums_ref, pick_ref, owner, rows):
    out_ref[:rows, :] = sums_ref[pl.ds(pl.multiple_of(owner * rows, rows), rows), :]
    out_ref[rows:, :] = jnp.dot(pick_ref[owner], sums_ref[...], preferred_element_type=F32).astype(BF16)


def first_layer_kernel(
    cuts, far, owners_hbm, count_hbm, bcount_hbm, x_hbm, wn_hbm, ws_hbm, deg_hbm, brow_hbm, ew_hbm, *rest
):
    outs, (sums_ref, pick_ref) = rest[: len(far)], rest[len(far) : len(far) + 2]
    owners_ref, count_ref, bcount_ref, brow_v, deg_v, x_v, wn_v, ws_v, ew_v, y_v, s_v, sems = rest[len(far) + 2 :]
    pairs = (
        (brow_hbm, brow_v),
        (owners_hbm, owners_ref),
        (x_hbm, x_v),
        (wn_hbm, wn_v),
        (count_hbm, count_ref),
        (bcount_hbm, bcount_ref),
        (deg_hbm, deg_v),
        (ws_hbm, ws_v),
        (ew_hbm, ew_v),
    )
    brow_in, owners_in, x_in, wn_in, *counts_in, deg_in, ws_in, ew_in = start_all(pairs, sems)
    _, _, neigh, cap, rows = ew_v.shape
    total = cuts * rows
    me = lax.axis_index("cuts")
    lane = lax.broadcasted_iota(jnp.int32, (cap, total), 1)
    eye = (
        lax.broadcasted_iota(jnp.int32, (cap, cap), 0) == lax.broadcasted_iota(jnp.int32, (cap, cap), 1)
    ).astype(F32)
    brow_in.wait()
    owners_in.wait()
    for k in range(neigh):
        columns = contract_last(eye, brow_v[0, k].astype(F32)).astype(jnp.int32)
        for u in range(cuts):
            target = columns[:, u : u + 1] + owners_ref[k, 0, u] * rows
            pick_ref[u, k * cap : (k + 1) * cap, :] = (lane == target).astype(F32).astype(BF16)
    x_in.wait()
    wn_in.wait()
    y_v[...] = jnp.dot(x_v[...], wn_v[...], preferred_element_type=F32).astype(BF16)
    ws_in.wait()
    s_v[...] = jnp.dot(x_v[...], ws_v[...], preferred_element_type=F32)
    for copy in (*counts_in, deg_in, ew_in):
        copy.wait()
    for u in range(cuts):
        at = slice(u * rows, (u + 1) * rows)
        picked = jnp.dot(pick_ref[u], y_v[...], preferred_element_type=F32).astype(BF16)
        summed = contract_first(live_tile(ew_v[0, u], count_ref, bcount_ref, u), picked)
        scale = as_column(1.0 / deg_v[:, at].astype(F32))
        sums_ref[at, :] = (s_v[at, :] + summed * scale).astype(BF16)
    for step, out_ref in zip(far, outs):
        fill_slab(out_ref, sums_ref, pick_ref, partner(me, step, cuts), rows)


def near_kernel(
    cuts,
    reps,
    subs,
    near,
    sums_ref,
    pick_ref,
    count_hbm,
    bcount_hbm,
    ws_hbm,
    wn_hbm,
    b1_hbm,
    b2_hbm,
    deg_hbm,
    ew_hbm,
    id_hbm,
    *rest,
):
    outs, rest = rest[: len(near)], rest[len(near) :]
    w_ref, b1_ref, b2_ref, live_ref, scale_ref, chosen_ref, slots_ref = rest[:7]
    count_ref, bcount_ref, deg_v, ew_v, id_v, sems = rest[7:]
    units = ws_hbm.shape[0]
    rows = ew_v.shape[2]
    me = lax.axis_index("cuts")
    pairs = (
        (count_hbm, count_ref),
        (bcount_hbm, bcount_ref),
        (deg_hbm, deg_v),
        (id_hbm, id_v),
        (ew_hbm.at[0, me], ew_v),
        (b1_hbm, b1_ref),
        (b2_hbm, b2_ref),
        (ws_hbm, w_ref.at[pl.ds(0, units)]),
        (wn_hbm, w_ref.at[pl.ds(units, units)]),
    )
    copies = start_all(pairs, sems)
    for step, out_ref in zip(near, outs):
        fill_slab(out_ref, sums_ref, pick_ref, partner(me, step, cuts), rows)
    for copy in copies[:5]:
        copy.wait()
    live_ref[...] = live_tile(ew_v[...], count_ref, bcount_ref, me)
    degrees = deg_v[:, pl.ds(pl.multiple_of(me * rows, rows), rows)].astype(F32)
    scale_ref[...] = jnp.broadcast_to(as_column(1.0 / degrees), (rows, rows))
    ids = id_v[...]
    device = ids // rows
    peer = (device // (reps * subs)) * reps + (device // subs) % reps
    slot = (ids - device * rows).astype(F32)
    peer_f = peer.astype(F32)
    down = lax.broadcasted_iota(jnp.int32, (rows, rows), 0)
    across = lax.broadcasted_iota(jnp.int32, (rows, rows), 1)
    earlier = (as_column(peer_f) == peer_f) & (down < across)
    rank = jnp.sum(earlier.astype(F32), axis=0, keepdims=True).astype(jnp.int32)
    place = peer * (rows // (cuts * reps)) + rank
    chosen = down == place
    chosen_ref[...] = chosen.astype(F32).astype(BF16)
    slots = jnp.sum(jnp.where(chosen, slot, 0.0), axis=1, keepdims=True)
    slots_ref[...] = jnp.broadcast_to(slots, (rows, rows)).astype(BF16)
    for copy in copies[5:]:
        copy.wait()


def second_layer_kernel(cuts, *rest):
    slabs = rest[:cuts]
    w_ref, b1_ref, b2_ref, live_ref, scale_ref, chosen_ref, slots_ref, out_ref = rest[cuts:]
    rows = chosen_ref.shape[0]
    units = w_ref.shape[1]
    total = slabs[0][...].astype(F32)
    for slab in slabs[1:]:
        total = total + slab[...].astype(F32)
    hidden = jnp.maximum(total + b1_ref[...], 0.0).astype(BF16)
    own, border = hidden[:rows], hidden[rows:]
    summed = contract_first(live_ref[...], border)
    mean = (summed * scale_ref[:, :1]).astype(BF16)
    z = jnp.dot(jnp.concatenate([own, mean], axis=1), w_ref[...], preferred_element_type=F32) + b2_ref[...]
    scale = lax.rsqrt(jnp.mean(z * z, axis=1, keepdims=True) + 1e-05)
    normalized = (z * scale).astype(BF16)
    out_ref[:, :units] = jnp.dot(chosen_ref[...], normalized, preferred_element_type=F32).astype(BF16)
    out_ref[:, units:] = slots_ref[...]


def placing_kernel(in_ref, out_ref):
    rows, units = out_ref.shape
    across = lax.broadcasted_iota(jnp.int32, (rows, rows), 1)
    chosen = in_ref[:, units:].astype(F32).astype(jnp.int32) == across
    out_ref[...] = contract_first(chosen.astype(F32).astype(BF16), in_ref[:, :units]).astype(BF16)


def body(
    features,
    w_self1,
    w_neigh1,
    bias1,
    w_self2,
    w_neigh2,
    bias2,
    degree,
    neighbor_owners,
    neighbor_count,
    boundary_rows,
    boundary_count,
    edge_weight,
    node_id,
):
    cuts, reps, subs = (lax.axis_size(a) for a in ("cuts", "rep", "sub"))
    total, width = features.shape
    units = w_self1.shape[1]
    _, _, neigh, cap, rows = edge_weight.shape
    border = neigh * cap
    vmem = pl.BlockSpec(memory_space=VMEM)
    hbm = pl.BlockSpec(memory_space=pltpu.HBM)
    shape = jax.ShapeDtypeStruct
    slab = shape((rows + border, units), BF16)
    near, far = list(range(min(2, cuts))), list(range(2, cuts))
    owners = neighbor_owners.transpose(2, 0, 1)
    bcounts = boundary_count.transpose(2, 0, 1)
    brows = boundary_rows.transpose(0, 2, 1, 3)
    counts_held = [SMEM(a.shape, jnp.int32) for a in (owners, neighbor_count, bcounts)]
    held = 2 * (total * width + 2 * width * units + cuts * border * total + 4 * total * units)
    held += 2 * cuts * (rows + border) * units + 8 * total * units + 2 * cuts * border * rows
    *sent_far, sums, pick = pl.pallas_call(
        functools.partial(first_layer_kernel, cuts, far),
        out_shape=[slab] * len(far) + [shape((total, units), BF16), shape((cuts, border, total), BF16)],
        in_specs=[hbm] * 9,
        out_specs=[vmem] * (len(far) + 2),
        scratch_shapes=[
            *counts_held,
            pltpu.VMEM(brows.shape, jnp.int32),
            pltpu.VMEM(degree.shape, jnp.int32),
            pltpu.VMEM((total, width), BF16),
            pltpu.VMEM((width, units), BF16),
            pltpu.VMEM((width, units), BF16),
            pltpu.VMEM(edge_weight.shape, BF16),
            pltpu.VMEM((total, units), BF16),
            pltpu.VMEM((total, units), F32),
            pltpu.SemaphoreType.DMA((9,)),
        ],
        compiler_params=pltpu.CompilerParams(vmem_limit_bytes=held + (8 << 20)),
        name="first_layer",
    )(*in_hbm(owners, neighbor_count, bcounts, features, w_neigh1, w_self1, degree, brows, edge_weight))
    *sent_near, weights, b1, b2, live, scale, chosen, slots = pl.pallas_call(
        functools.partial(near_kernel, cuts, reps, subs, near),
        out_shape=[slab] * len(near)
        + [
            shape((2 * units, units), BF16),
            shape((1, units), F32),
            shape((1, units), F32),
            shape((border, rows), BF16),
            shape((rows, rows), F32),
            shape((rows, rows), BF16),
            shape((rows, rows), BF16),
        ],
        in_specs=[vmem] * 2 + [hbm] * 9,
        out_specs=[vmem] * (len(near) + 7),
        scratch_shapes=[
            *counts_held[1:],
            pltpu.VMEM(degree.shape, jnp.int32),
            pltpu.VMEM(edge_weight.shape[2:], BF16),
            pltpu.VMEM(node_id.shape, jnp.int32),
            pltpu.SemaphoreType.DMA((9,)),
        ],
        compiler_params=pltpu.CompilerParams(vmem_limit_bytes=held + (8 << 20)),
        cost_estimate=pl.CostEstimate(flops=2 * border * total * units, bytes_accessed=4 * units * units, transcendentals=0),
        name="near_slabs",
    )(
        sums,
        pick,
        *in_hbm(neighbor_count, bcounts, w_self2, w_neigh2, bias1.reshape(1, units), bias2.reshape(1, units)),
        *in_hbm(degree, edge_weight, node_id),
    )
    sent = dict(zip(near + far, sent_near + sent_far))
    arrived = [sent[s] if s == 0 else lax.ppermute(sent[s], "cuts", partner_pairs(s, cuts)) for s in range(cuts)]
    payload = pl.pallas_call(
        functools.partial(second_layer_kernel, cuts),
        out_shape=shape((rows, units + rows), BF16),
        in_specs=[vmem] * (cuts + 7),
        out_specs=vmem,
        compiler_params=pltpu.CompilerParams(vmem_limit_bytes=24 << 20),
        name="second_layer",
    )(*arrived, weights, b1, b2, live, scale, chosen, slots)
    peers = cuts * reps
    moved = lax.all_to_all(
        payload.reshape(peers, rows // peers, units + rows), ("cuts", "rep"), split_axis=0, concat_axis=0, tiled=True
    )
    return pl.pallas_call(
        placing_kernel,
        out_shape=shape((rows, units), BF16),
        in_specs=[vmem],
        out_specs=vmem,
        name="placing",
    )(moved.reshape(rows, units + rows))


def solution(mesh):
    block = ("groups", "rep", "sub")
    placed = (
        P(block, "cuts"),
        P("cuts", None),
        P("cuts", None),
        P(),
        P(),
        P(),
        P(),
        P(block, None),
        P(block, None, None),
        P(block, None),
        P(block, None, None, None),
        P(block, None, None),
        P(block, None, None, None, None),
        P(block, "cuts"),
    )
    return jax.shard_map(
        body,
        mesh=mesh,
        in_specs=placed,
        out_specs=P(("groups", "cuts", "rep", "sub"), None),
        check_vma=False,
    )
```

```python
import functools

import jax
import jax.numpy as jnp
from jax import lax
from jax.experimental import pallas as pl
from jax.experimental.pallas import tpu as pltpu
from jax.sharding import PartitionSpec as P

F32 = jnp.float32
BF16 = jnp.bfloat16
VMEM = pltpu.VMEM
SMEM = pltpu.SMEM


def partner_pairs(step, total):
    return [(i, i ^ step) for i in range(total)]


def as_column(row):
    n = row.shape[1]
    eye = lax.broadcasted_iota(jnp.int32, (n, n), 0) == lax.broadcasted_iota(jnp.int32, (n, n), 1)
    return jnp.sum(jnp.where(eye, jnp.broadcast_to(row, (n, n)), 0.0), axis=1, keepdims=True)


def live_limit(count_ref, bcount_ref, owner, k):
    return jnp.where(k < count_ref[0, owner], bcount_ref[k, 0, owner], 0)


def live_tile(tile, count_ref, bcount_ref, owner):
    neigh, cap, rows = tile.shape
    slot = lax.broadcasted_iota(jnp.int32, (cap, rows), 0)
    tiles = []
    for k in range(neigh):
        live = slot < live_limit(count_ref, bcount_ref, owner, k)
        tiles.append(jnp.where(live, tile[k].astype(F32), 0.0).astype(BF16))
    return jnp.concatenate(tiles, axis=0)


def contract_first(a, b):
    return lax.dot_general(a, b, (((0,), (0,)), ((), ())), preferred_element_type=F32)


def contract_last(a, b):
    return lax.dot_general(a, b, (((1,), (1,)), ((), ())), preferred_element_type=F32)


def in_hbm(*arrays):
    return [pltpu.with_memory_space_constraint(a, pltpu.HBM) for a in arrays]


def start_all(pairs, sems):
    copies = [pltpu.make_async_copy(src, dst, sems.at[i]) for i, (src, dst) in enumerate(pairs)]
    for copy in copies:
        copy.start()
    return copies


def own_part(sums_ref, owner, rows):
    return sums_ref[pl.ds(pl.multiple_of(owner * rows, rows), rows), :]


def border_part(sums_ref, pick_ref, owner):
    return jnp.dot(pick_ref[owner], sums_ref[...], preferred_element_type=F32)


def first_layer_kernel(
    cuts, owners_hbm, count_hbm, bcount_hbm, x_hbm, wn_hbm, ws_hbm, deg_hbm, brow_hbm, ew_hbm, *rest
):
    near, far = min(2, cuts), cuts - min(2, cuts)
    border_refs, own_refs, slab_refs, local_refs = (
        rest[: far // 2],
        rest[far // 2 : far // 2 + far],
        rest[far // 2 + far : far // 2 + far + near],
        rest[far // 2 + far + near : 2 * far + near],
    )
    rest = rest[2 * far + near :]
    owners_ref, count_ref, bcount_ref, brow_v, deg_v, x_v, wn_v, ws_v, ew_v, pick_v, y_v, s_v, sums_v, sems = rest
    pairs = (
        (brow_hbm, brow_v),
        (owners_hbm, owners_ref),
        (x_hbm, x_v),
        (wn_hbm, wn_v),
        (count_hbm, count_ref),
        (bcount_hbm, bcount_ref),
        (deg_hbm, deg_v),
        (ws_hbm, ws_v),
        (ew_hbm, ew_v),
    )
    brow_in, owners_in, x_in, wn_in, *counts_in, deg_in, ws_in, ew_in = start_all(pairs, sems)
    _, _, neigh, cap, rows = ew_v.shape
    total = cuts * rows
    me = lax.axis_index("cuts")
    lane = lax.broadcasted_iota(jnp.int32, (cap, total), 1)
    eye = (
        lax.broadcasted_iota(jnp.int32, (cap, cap), 0) == lax.broadcasted_iota(jnp.int32, (cap, cap), 1)
    ).astype(F32)
    brow_in.wait()
    owners_in.wait()
    for k in range(neigh):
        columns = contract_last(eye, brow_v[0, k].astype(F32)).astype(jnp.int32)
        for u in range(cuts):
            target = columns[:, u : u + 1] + owners_ref[k, 0, u] * rows
            pick_v[u, k * cap : (k + 1) * cap, :] = (lane == target).astype(F32).astype(BF16)
    x_in.wait()
    wn_in.wait()
    y_v[...] = jnp.dot(x_v[...], wn_v[...], preferred_element_type=F32).astype(BF16)
    ws_in.wait()
    s_v[...] = jnp.dot(x_v[...], ws_v[...], preferred_element_type=F32)
    for copy in (*counts_in, deg_in, ew_in):
        copy.wait()
    for u in range(cuts):
        at = slice(u * rows, (u + 1) * rows)
        picked = jnp.dot(pick_v[u], y_v[...], preferred_element_type=F32).astype(BF16)
        summed = contract_first(live_tile(ew_v[0, u], count_ref, bcount_ref, u), picked)
        scale = as_column(1.0 / deg_v[:, at].astype(F32))
        sums_v[at, :] = (s_v[at, :] + summed * scale).astype(BF16)
    for i, out_ref in enumerate(border_refs):
        out_ref[...] = border_part(sums_v, pick_v, me ^ (2 * i + 3)).astype(BF16)
    for i, out_ref in enumerate(own_refs):
        out_ref[...] = own_part(sums_v, me ^ (i + 2), rows)
    for step, out_ref in enumerate(slab_refs):
        out_ref[:rows, :] = own_part(sums_v, me ^ step, rows)
        out_ref[rows:, :] = border_part(sums_v, pick_v, me ^ step).astype(BF16)
    for i, out_ref in enumerate(local_refs):
        out_ref[...] = border_part(sums_v, pick_v, me ^ (2 * i + 2))


def hidden_rows(parts, b1_ref):
    total = parts[0].astype(F32)
    for part in parts[1:]:
        total = total + part.astype(F32)
    return jnp.maximum(total + b1_ref[...], 0.0).astype(BF16)


def own_rows_kernel(cuts, reps, subs, *rest):
    near, far = min(2, cuts), cuts - min(2, cuts)
    slab_refs, own_refs, rest = rest[:near], rest[near : near + far], rest[near + far :]
    count_hbm, bcount_hbm, ws_hbm, wn_hbm, b1_hbm, b2_hbm, deg_hbm, ew_hbm, id_hbm = rest[:9]
    z_ref, wn_ref, b1_ref, live_ref, scale_ref, chosen_ref, slots_ref = rest[9:16]
    ws_v, b2_v, count_ref, bcount_ref, deg_v, ew_v, id_v, sems = rest[16:]
    rows = ew_v.shape[2]
    me = lax.axis_index("cuts")
    pairs = (
        (count_hbm, count_ref),
        (bcount_hbm, bcount_ref),
        (deg_hbm, deg_v),
        (id_hbm, id_v),
        (ew_hbm.at[0, me], ew_v),
        (b1_hbm, b1_ref),
        (b2_hbm, b2_v),
        (ws_hbm, ws_v),
        (wn_hbm, wn_ref),
    )
    copies = start_all(pairs, sems)
    for copy in copies[:5]:
        copy.wait()
    live_ref[...] = live_tile(ew_v[...], count_ref, bcount_ref, me)
    degrees = deg_v[:, pl.ds(pl.multiple_of(me * rows, rows), rows)].astype(F32)
    scale_ref[...] = jnp.broadcast_to(as_column(1.0 / degrees), (rows, rows))
    ids = id_v[...]
    device = ids // rows
    peer = (device // (reps * subs)) * reps + (device // subs) % reps
    slot = (ids - device * rows).astype(F32)
    peer_f = peer.astype(F32)
    down = lax.broadcasted_iota(jnp.int32, (rows, rows), 0)
    across = lax.broadcasted_iota(jnp.int32, (rows, rows), 1)
    earlier = (as_column(peer_f) == peer_f) & (down < across)
    rank = jnp.sum(earlier.astype(F32), axis=0, keepdims=True).astype(jnp.int32)
    place = peer * (rows // (cuts * reps)) + rank
    chosen = down == place
    chosen_ref[...] = chosen.astype(F32).astype(BF16)
    slots = jnp.sum(jnp.where(chosen, slot, 0.0), axis=1, keepdims=True)
    slots_ref[...] = jnp.broadcast_to(slots, (rows, rows)).astype(BF16)
    for copy in copies[5:]:
        copy.wait()
    own = hidden_rows([slab[:rows, :] for slab in slab_refs] + [part[...] for part in own_refs], b1_ref)
    z_ref[...] = jnp.dot(own, ws_v[...], preferred_element_type=F32) + b2_v[...]


def border_rows_kernel(cuts, *rest):
    near, far = min(2, cuts), cuts - min(2, cuts)
    slab_refs, border_refs, rest = rest[:near], rest[near : near + far // 2], rest[near + far // 2 :]
    z_ref, wn_ref, b1_ref, live_ref, scale_ref, chosen_ref, slots_ref, out_ref = rest
    rows = chosen_ref.shape[0]
    units = wn_ref.shape[1]
    border = hidden_rows([slab[rows:, :] for slab in slab_refs] + [part[...] for part in border_refs], b1_ref)
    summed = contract_first(live_ref[...], border)
    mean = (summed * scale_ref[:, :1]).astype(BF16)
    z = z_ref[...] + jnp.dot(mean, wn_ref[...], preferred_element_type=F32)
    scale = lax.rsqrt(jnp.mean(z * z, axis=1, keepdims=True) + 1e-05)
    normalized = (z * scale).astype(BF16)
    out_ref[:, :units] = jnp.dot(chosen_ref[...], normalized, preferred_element_type=F32).astype(BF16)
    out_ref[:, units:] = slots_ref[...]


def placing_kernel(in_ref, out_ref):
    rows, units = out_ref.shape
    across = lax.broadcasted_iota(jnp.int32, (rows, rows), 1)
    chosen = in_ref[:, units:].astype(F32).astype(jnp.int32) == across
    out_ref[...] = contract_first(chosen.astype(F32).astype(BF16), in_ref[:, :units]).astype(BF16)


def body(
    features,
    w_self1,
    w_neigh1,
    bias1,
    w_self2,
    w_neigh2,
    bias2,
    degree,
    neighbor_owners,
    neighbor_count,
    boundary_rows,
    boundary_count,
    edge_weight,
    node_id,
):
    cuts, reps, subs = (lax.axis_size(a) for a in ("cuts", "rep", "sub"))
    total, width = features.shape
    units = w_self1.shape[1]
    _, _, neigh, cap, rows = edge_weight.shape
    border = neigh * cap
    vmem = pl.BlockSpec(memory_space=VMEM)
    hbm = pl.BlockSpec(memory_space=pltpu.HBM)
    shape = jax.ShapeDtypeStruct
    slab = shape((rows + border, units), BF16)
    own_slab, border_slab = shape((rows, units), BF16), shape((border, units), BF16)
    near, far = min(2, cuts), cuts - min(2, cuts)
    owners = neighbor_owners.transpose(2, 0, 1)
    bcounts = boundary_count.transpose(2, 0, 1)
    brows = boundary_rows.transpose(0, 2, 1, 3)
    counts_held = [SMEM(a.shape, jnp.int32) for a in (owners, neighbor_count, bcounts)]
    held = 2 * (total * width + 2 * width * units + cuts * border * total + 4 * total * units)
    held += 2 * cuts * (rows + border) * units + 8 * total * units + 2 * cuts * border * rows
    sent = pl.pallas_call(
        functools.partial(first_layer_kernel, cuts),
        out_shape=[border_slab] * (far // 2)
        + [own_slab] * far
        + [slab] * near
        + [shape((border, units), F32)] * (far // 2),
        in_specs=[hbm] * 9,
        out_specs=[vmem] * (2 * far + near),
        scratch_shapes=[
            *counts_held,
            pltpu.VMEM(brows.shape, jnp.int32),
            pltpu.VMEM(degree.shape, jnp.int32),
            pltpu.VMEM((total, width), BF16),
            pltpu.VMEM((width, units), BF16),
            pltpu.VMEM((width, units), BF16),
            pltpu.VMEM(edge_weight.shape, BF16),
            pltpu.VMEM((cuts, border, total), BF16),
            pltpu.VMEM((total, units), BF16),
            pltpu.VMEM((total, units), F32),
            pltpu.VMEM((total, units), BF16),
            pltpu.SemaphoreType.DMA((9,)),
        ],
        compiler_params=pltpu.CompilerParams(vmem_limit_bytes=held + (8 << 20)),
        name="first_layer",
    )(*in_hbm(owners, neighbor_count, bcounts, features, w_neigh1, w_self1, degree, brows, edge_weight))
    sent = list(sent)
    pairs, owns, slabs, local = (
        sent[: far // 2],
        sent[far // 2 : far // 2 + far],
        sent[far // 2 + far : far // 2 + far + near],
        sent[far // 2 + far + near :],
    )
    trade = lambda a, step: lax.ppermute(a, "cuts", partner_pairs(step, cuts))
    pairs = [trade(a, 1) for a in pairs]
    owns = [trade(a, i + 2) for i, a in enumerate(owns)]
    slabs = slabs[:1] + [trade(a, 1) for a in slabs[1:]]
    paired = [(a + b.astype(F32)).astype(BF16) for a, b in zip(local, pairs)]
    borders = [trade(a, 2 * i + 2) for i, a in enumerate(paired)]
    prepared = pl.pallas_call(
        functools.partial(own_rows_kernel, cuts, reps, subs),
        out_shape=[
            shape((rows, units), F32),
            shape((units, units), BF16),
            shape((1, units), F32),
            shape((border, rows), BF16),
            shape((rows, rows), F32),
            shape((rows, rows), BF16),
            shape((rows, rows), BF16),
        ],
        in_specs=[vmem] * cuts + [hbm] * 9,
        out_specs=[vmem] * 7,
        scratch_shapes=[
            pltpu.VMEM((units, units), BF16),
            pltpu.VMEM((1, units), F32),
            *counts_held[1:],
            pltpu.VMEM(degree.shape, jnp.int32),
            pltpu.VMEM(edge_weight.shape[2:], BF16),
            pltpu.VMEM(node_id.shape, jnp.int32),
            pltpu.SemaphoreType.DMA((9,)),
        ],
        compiler_params=pltpu.CompilerParams(vmem_limit_bytes=24 << 20),
        cost_estimate=pl.CostEstimate(flops=2 * rows * units * units, bytes_accessed=4 * units * units, transcendentals=0),
        name="own_rows",
    )(
        *slabs,
        *owns,
        *in_hbm(neighbor_count, bcounts, w_self2, w_neigh2, bias1.reshape(1, units), bias2.reshape(1, units)),
        *in_hbm(degree, edge_weight, node_id),
    )
    payload = pl.pallas_call(
        functools.partial(border_rows_kernel, cuts),
        out_shape=shape((rows, units + rows), BF16),
        in_specs=[vmem] * (near + far // 2 + 7),
        out_specs=vmem,
        compiler_params=pltpu.CompilerParams(vmem_limit_bytes=24 << 20),
        name="border_rows",
    )(*slabs, *borders, *prepared)
    peers = cuts * reps
    moved = lax.all_to_all(
        payload.reshape(peers, rows // peers, units + rows), ("cuts", "rep"), split_axis=0, concat_axis=0, tiled=True
    )
    return pl.pallas_call(
        placing_kernel,
        out_shape=shape((rows, units), BF16),
        in_specs=[vmem],
        out_specs=vmem,
        name="placing",
    )(moved.reshape(rows, units + rows))


def solution(mesh):
    block = ("groups", "rep", "sub")
    placed = (
        P(block, "cuts"),
        P("cuts", None),
        P("cuts", None),
        P(),
        P(),
        P(),
        P(),
        P(block, None),
        P(block, None, None),
        P(block, None),
        P(block, None, None, None),
        P(block, None, None),
        P(block, None, None, None, None),
        P(block, "cuts"),
    )
    return jax.shard_map(
        body,
        mesh=mesh,
        in_specs=placed,
        out_specs=P(("groups", "cuts", "rep", "sub"), None),
        check_vma=False,
    )
```

```python
import functools

import jax
import jax.numpy as jnp
from jax import lax
from jax.experimental import pallas as pl
from jax.experimental.pallas import tpu as pltpu
from jax.sharding import PartitionSpec as P

F32 = jnp.float32
BF16 = jnp.bfloat16
VMEM = pltpu.VMEM
SMEM = pltpu.SMEM


def partner_pairs(step, total):
    return [(i, i ^ step) for i in range(total)]


def as_column(row):
    n = row.shape[1]
    eye = lax.broadcasted_iota(jnp.int32, (n, n), 0) == lax.broadcasted_iota(jnp.int32, (n, n), 1)
    return jnp.sum(jnp.where(eye, jnp.broadcast_to(row, (n, n)), 0.0), axis=1, keepdims=True)


def live_limit(count_ref, bcount_ref, owner, k):
    return jnp.where(k < count_ref[0, owner], bcount_ref[k, 0, owner], 0)


def live_tile(tile, count_ref, bcount_ref, owner):
    neigh, cap, rows = tile.shape
    slot = lax.broadcasted_iota(jnp.int32, (cap, rows), 0)
    tiles = []
    for k in range(neigh):
        live = slot < live_limit(count_ref, bcount_ref, owner, k)
        tiles.append(jnp.where(live, tile[k].astype(F32), 0.0).astype(BF16))
    return jnp.concatenate(tiles, axis=0)


def contract_first(a, b):
    return lax.dot_general(a, b, (((0,), (0,)), ((), ())), preferred_element_type=F32)


def contract_last(a, b):
    return lax.dot_general(a, b, (((1,), (1,)), ((), ())), preferred_element_type=F32)


def in_hbm(*arrays):
    return [pltpu.with_memory_space_constraint(a, pltpu.HBM) for a in arrays]


def start_all(pairs, sems):
    copies = [pltpu.make_async_copy(src, dst, sems.at[i]) for i, (src, dst) in enumerate(pairs)]
    for copy in copies:
        copy.start()
    return copies


def part_of(ref, owner, size):
    return ref[pl.ds(pl.multiple_of(owner * size, size), size), :]


def first_layer_kernel(
    cuts, owners_hbm, count_hbm, bcount_hbm, x_hbm, wn_hbm, ws_hbm, deg_hbm, brow_hbm, ew_hbm, *rest
):
    near, far = min(2, cuts), cuts - min(2, cuts)
    border_refs, own_refs, slab_refs, local_refs = (
        rest[: far // 2],
        rest[far // 2 : far // 2 + far],
        rest[far // 2 + far : far // 2 + far + near],
        rest[far // 2 + far + near : 2 * far + near],
    )
    rest = rest[2 * far + near :]
    owners_ref, count_ref, bcount_ref, brow_v, deg_v, x_v, wn_v, ws_v, ew_v, pick_v, adj_v, *rest = rest
    scale_v, y_v, sums_v, border_v, sems = rest
    pairs = (
        (brow_hbm, brow_v),
        (owners_hbm, owners_ref),
        (count_hbm, count_ref),
        (bcount_hbm, bcount_ref),
        (deg_hbm, deg_v),
        (ew_hbm, ew_v),
        (x_hbm, x_v),
        (wn_hbm, wn_v),
        (ws_hbm, ws_v),
    )
    brow_in, owners_in, *counts_in, deg_in, ew_in, x_in, wn_in, ws_in = start_all(pairs, sems)
    _, _, neigh, cap, rows = ew_v.shape
    total = cuts * rows
    me = lax.axis_index("cuts")
    lane = lax.broadcasted_iota(jnp.int32, (cap, total), 1)
    eye = (
        lax.broadcasted_iota(jnp.int32, (cap, cap), 0) == lax.broadcasted_iota(jnp.int32, (cap, cap), 1)
    ).astype(F32)
    span = min(cuts, 4)

    def fill_picks(first):
        for k in range(neigh):
            columns = contract_last(eye, brow_v[0, k].astype(F32)).astype(jnp.int32)
            for u in range(span):
                target = columns[:, first + u : first + u + 1] + owners_ref[k, 0, first + u] * rows
                at = u * neigh * cap + k * cap
                pick_v[at : at + cap, :] = (lane == target).astype(F32).astype(BF16)

    brow_in.wait()
    owners_in.wait()
    for first in range(0, cuts, span):
        fill_picks(first)
        if first == 0:
            for copy in (*counts_in, deg_in, ew_in):
                copy.wait()
        for u in range(first, first + span):
            at = slice(u * rows, (u + 1) * rows)
            picks = pick_v[(u - first) * neigh * cap : (u - first + 1) * neigh * cap, :]
            adj_v[at, :] = contract_first(live_tile(ew_v[0, u], count_ref, bcount_ref, u), picks).astype(BF16)
            scale_v[at, :] = as_column(1.0 / deg_v[:, at].astype(F32))
    x_in.wait()
    wn_in.wait()
    for first in range(0, cuts, span):
        at = slice(first * rows, (first + span) * rows)
        y_v[at, :] = jnp.dot(x_v[at, :], wn_v[...], preferred_element_type=F32).astype(BF16)
    ws_in.wait()
    for first in range(0, cuts, span):
        at = slice(first * rows, (first + span) * rows)
        selfs = jnp.dot(x_v[at, :], ws_v[...], preferred_element_type=F32)
        summed = jnp.dot(adj_v[at, :], y_v[...], preferred_element_type=F32)
        sums_v[at, :] = (selfs + summed * scale_v[at, :]).astype(BF16)
    for first in range(0, cuts, span):
        if span < cuts:
            fill_picks(first)
        at = slice(first * neigh * cap, (first + span) * neigh * cap)
        border_v[at, :] = jnp.dot(pick_v[...], sums_v[...], preferred_element_type=F32).astype(BF16)
    for i, out_ref in enumerate(border_refs):
        out_ref[...] = part_of(border_v, me ^ (2 * i + 3), neigh * cap)
    for i, out_ref in enumerate(own_refs):
        out_ref[...] = part_of(sums_v, me ^ (i + 2), rows)
    for step, out_ref in enumerate(slab_refs):
        out_ref[:rows, :] = part_of(sums_v, me ^ step, rows)
        out_ref[rows:, :] = part_of(border_v, me ^ step, neigh * cap)
    for i, out_ref in enumerate(local_refs):
        out_ref[...] = part_of(border_v, me ^ (2 * i + 2), neigh * cap)


def hidden_rows(parts, b1_ref):
    total = parts[0].astype(F32)
    for part in parts[1:]:
        total = total + part.astype(F32)
    return jnp.maximum(total + b1_ref[...], 0.0).astype(BF16)


def prepare_kernel(cuts, reps, subs, after_ref, *rest):
    count_hbm, bcount_hbm, ws_hbm, wn_hbm, b1_hbm, b2_hbm, deg_hbm, ew_hbm, id_hbm = rest[:9]
    w_ref, b1_ref, b2_ref, live_ref, scale_ref, chosen_ref, slots_ref = rest[9:16]
    count_ref, bcount_ref, deg_v, ew_v, id_v, sems = rest[16:]
    units = ws_hbm.shape[0]
    rows = ew_v.shape[2]
    me = lax.axis_index("cuts")
    pairs = (
        (count_hbm, count_ref),
        (bcount_hbm, bcount_ref),
        (deg_hbm, deg_v),
        (id_hbm, id_v),
        (ew_hbm.at[0, me], ew_v),
        (b1_hbm, b1_ref),
        (b2_hbm, b2_ref),
        (ws_hbm, w_ref.at[pl.ds(0, units)]),
        (wn_hbm, w_ref.at[pl.ds(units, units)]),
    )
    copies = start_all(pairs, sems)
    for copy in copies[:5]:
        copy.wait()
    live_ref[...] = live_tile(ew_v[...], count_ref, bcount_ref, me)
    degrees = deg_v[:, pl.ds(pl.multiple_of(me * rows, rows), rows)].astype(F32)
    scale_ref[...] = jnp.broadcast_to(as_column(1.0 / degrees), (rows, rows))
    ids = id_v[...]
    device = ids // rows
    peer = (device // (reps * subs)) * reps + (device // subs) % reps
    slot = (ids - device * rows).astype(F32)
    peer_f = peer.astype(F32)
    down = lax.broadcasted_iota(jnp.int32, (rows, rows), 0)
    across = lax.broadcasted_iota(jnp.int32, (rows, rows), 1)
    earlier = (as_column(peer_f) == peer_f) & (down < across)
    rank = jnp.sum(earlier.astype(F32), axis=0, keepdims=True).astype(jnp.int32)
    place = peer * (rows // (cuts * reps)) + rank
    chosen = down == place
    chosen_ref[...] = chosen.astype(F32).astype(BF16)
    slots = jnp.sum(jnp.where(chosen, slot, 0.0), axis=1, keepdims=True)
    slots_ref[...] = jnp.broadcast_to(slots, (rows, rows)).astype(BF16)
    for copy in copies[5:]:
        copy.wait()


def second_layer_kernel(cuts, *rest):
    near, far = min(2, cuts), cuts - min(2, cuts)
    slab_refs, own_refs, border_refs = rest[:near], rest[near : near + far], rest[near + far : near + far + far // 2]
    w_ref, b1_ref, b2_ref, live_ref, scale_ref, chosen_ref, slots_ref, out_ref = rest[near + far + far // 2 :]
    rows = chosen_ref.shape[0]
    units = w_ref.shape[1]
    own = hidden_rows([slab[:rows, :] for slab in slab_refs] + [part[...] for part in own_refs], b1_ref)
    border = hidden_rows([slab[rows:, :] for slab in slab_refs] + [part[...] for part in border_refs], b1_ref)
    summed = contract_first(live_ref[...], border)
    mean = (summed * scale_ref[:, :1]).astype(BF16)
    z = jnp.dot(jnp.concatenate([own, mean], axis=1), w_ref[...], preferred_element_type=F32) + b2_ref[...]
    scale = lax.rsqrt(jnp.mean(z * z, axis=1, keepdims=True) + 1e-05)
    normalized = (z * scale).astype(BF16)
    out_ref[:, :units] = jnp.dot(chosen_ref[...], normalized, preferred_element_type=F32).astype(BF16)
    out_ref[:, units:] = slots_ref[...]


def placing_kernel(in_ref, out_ref):
    rows, units = out_ref.shape
    across = lax.broadcasted_iota(jnp.int32, (rows, rows), 1)
    chosen = in_ref[:, units:].astype(F32).astype(jnp.int32) == across
    out_ref[...] = contract_first(chosen.astype(F32).astype(BF16), in_ref[:, :units]).astype(BF16)


def body(
    features,
    w_self1,
    w_neigh1,
    bias1,
    w_self2,
    w_neigh2,
    bias2,
    degree,
    neighbor_owners,
    neighbor_count,
    boundary_rows,
    boundary_count,
    edge_weight,
    node_id,
):
    cuts, reps, subs = (lax.axis_size(a) for a in ("cuts", "rep", "sub"))
    total, width = features.shape
    units = w_self1.shape[1]
    _, _, neigh, cap, rows = edge_weight.shape
    border = neigh * cap
    vmem = pl.BlockSpec(memory_space=VMEM)
    hbm = pl.BlockSpec(memory_space=pltpu.HBM)
    shape = jax.ShapeDtypeStruct
    slab = shape((rows + border, units), BF16)
    own_slab, border_slab = shape((rows, units), BF16), shape((border, units), BF16)
    near, far = min(2, cuts), cuts - min(2, cuts)
    owners = neighbor_owners.transpose(2, 0, 1)
    bcounts = boundary_count.transpose(2, 0, 1)
    brows = boundary_rows.transpose(0, 2, 1, 3)
    counts_held = [SMEM(a.shape, jnp.int32) for a in (owners, neighbor_count, bcounts)]
    held = total * width + 2 * width * units + total * total + 2 * total * units + 256 * total
    held += min(cuts, 4) * border * total + cuts * border * (units + rows) + units * (near * (rows + border) + far * (rows + border))
    sent = pl.pallas_call(
        functools.partial(first_layer_kernel, cuts),
        out_shape=[border_slab] * (far // 2)
        + [own_slab] * far
        + [slab] * near
        + [border_slab] * (far // 2),
        in_specs=[hbm] * 9,
        out_specs=[vmem] * (2 * far + near),
        scratch_shapes=[
            *counts_held,
            pltpu.VMEM(brows.shape, jnp.int32),
            pltpu.VMEM(degree.shape, jnp.int32),
            pltpu.VMEM((total, width), BF16),
            pltpu.VMEM((width, units), BF16),
            pltpu.VMEM((width, units), BF16),
            pltpu.VMEM(edge_weight.shape, BF16),
            pltpu.VMEM((min(cuts, 4) * border, total), BF16),
            pltpu.VMEM((total, total), BF16),
            pltpu.VMEM((total, 1), F32),
            pltpu.VMEM((total, units), BF16),
            pltpu.VMEM((total, units), BF16),
            pltpu.VMEM((cuts * border, units), BF16),
            pltpu.SemaphoreType.DMA((9,)),
        ],
        compiler_params=pltpu.CompilerParams(vmem_limit_bytes=2 * held + (8 << 20)),
        name="first_layer",
    )(*in_hbm(owners, neighbor_count, bcounts, features, w_neigh1, w_self1, degree, brows, edge_weight))
    sent = list(sent)
    pairs, owns, slabs, local = (
        sent[: far // 2],
        sent[far // 2 : far // 2 + far],
        sent[far // 2 + far : far // 2 + far + near],
        sent[far // 2 + far + near :],
    )
    trade = lambda a, step: lax.ppermute(a, "cuts", partner_pairs(step, cuts))
    pairs = [trade(a, 1) for a in pairs]
    owns = [trade(a, i + 2) for i, a in enumerate(owns)]
    slabs = slabs[:1] + [trade(a, 1) for a in slabs[1:]]
    paired = [(a.astype(F32) + b.astype(F32)).astype(BF16) for a, b in zip(local, pairs)]
    borders = [trade(a, 2 * i + 2) for i, a in enumerate(paired)]
    prepared = pl.pallas_call(
        functools.partial(prepare_kernel, cuts, reps, subs),
        out_shape=[
            shape((2 * units, units), BF16),
            shape((1, units), F32),
            shape((1, units), F32),
            shape((border, rows), BF16),
            shape((rows, rows), F32),
            shape((rows, rows), BF16),
            shape((rows, rows), BF16),
        ],
        in_specs=[pl.BlockSpec(memory_space=pl.ANY)] + [hbm] * 9,
        out_specs=[vmem] * 7,
        scratch_shapes=[
            *counts_held[1:],
            pltpu.VMEM(degree.shape, jnp.int32),
            pltpu.VMEM(edge_weight.shape[2:], BF16),
            pltpu.VMEM(node_id.shape, jnp.int32),
            pltpu.SemaphoreType.DMA((9,)),
        ],
        compiler_params=pltpu.CompilerParams(vmem_limit_bytes=24 << 20),
        cost_estimate=pl.CostEstimate(flops=rows * rows * units, bytes_accessed=4 * units * units, transcendentals=0),
        name="prepare",
    )(
        sent[-1],
        *in_hbm(neighbor_count, bcounts, w_self2, w_neigh2, bias1.reshape(1, units), bias2.reshape(1, units)),
        *in_hbm(degree, edge_weight, node_id),
    )
    arrived = slabs + owns + borders
    payload = pl.pallas_call(
        functools.partial(second_layer_kernel, cuts),
        out_shape=shape((rows, units + rows), BF16),
        in_specs=[vmem] * (len(arrived) + 7),
        out_specs=vmem,
        compiler_params=pltpu.CompilerParams(vmem_limit_bytes=24 << 20),
        name="second_layer",
    )(*arrived, *prepared)
    peers = cuts * reps
    moved = lax.all_to_all(
        payload.reshape(peers, rows // peers, units + rows), ("cuts", "rep"), split_axis=0, concat_axis=0, tiled=True
    )
    return pl.pallas_call(
        placing_kernel,
        out_shape=shape((rows, units), BF16),
        in_specs=[vmem],
        out_specs=vmem,
        name="placing",
    )(moved.reshape(rows, units + rows))


def solution(mesh):
    block = ("groups", "rep", "sub")
    placed = (
        P(block, "cuts"),
        P("cuts", None),
        P("cuts", None),
        P(),
        P(),
        P(),
        P(),
        P(block, None),
        P(block, None, None),
        P(block, None),
        P(block, None, None, None),
        P(block, None, None),
        P(block, None, None, None, None),
        P(block, "cuts"),
    )
    return jax.shard_map(
        body,
        mesh=mesh,
        in_specs=placed,
        out_specs=P(("groups", "cuts", "rep", "sub"), None),
        check_vma=False,
    )
```

```python
import functools

import jax
import jax.numpy as jnp
from jax import lax
from jax.experimental import pallas as pl
from jax.experimental.pallas import tpu as pltpu
from jax.sharding import PartitionSpec as P

F32 = jnp.float32
BF16 = jnp.bfloat16
VMEM = pltpu.VMEM
SMEM = pltpu.SMEM
DIRECT = 112


def direct_rows(rows):
    return rows * DIRECT // 128


def partner_pairs(step, total):
    return [(i, i ^ step) for i in range(total)]


def as_column(row):
    n = row.shape[1]
    eye = lax.broadcasted_iota(jnp.int32, (n, n), 0) == lax.broadcasted_iota(jnp.int32, (n, n), 1)
    return jnp.sum(jnp.where(eye, jnp.broadcast_to(row, (n, n)), 0.0), axis=1, keepdims=True)


def live_limit(count_ref, bcount_ref, owner, k):
    return jnp.where(k < count_ref[0, owner], bcount_ref[k, 0, owner], 0)


def live_tile(tile, count_ref, bcount_ref, owner):
    neigh, cap, rows = tile.shape
    slot = lax.broadcasted_iota(jnp.int32, (cap, rows), 0)
    tiles = []
    for k in range(neigh):
        live = slot < live_limit(count_ref, bcount_ref, owner, k)
        tiles.append(jnp.where(live, tile[k].astype(F32), 0.0).astype(BF16))
    return jnp.concatenate(tiles, axis=0)


def contract_first(a, b):
    return lax.dot_general(a, b, (((0,), (0,)), ((), ())), preferred_element_type=F32)


def contract_last(a, b):
    return lax.dot_general(a, b, (((1,), (1,)), ((), ())), preferred_element_type=F32)


def in_hbm(*arrays):
    return [pltpu.with_memory_space_constraint(a, pltpu.HBM) for a in arrays]


def start_all(pairs, sems):
    copies = [pltpu.make_async_copy(src, dst, sems.at[i]) for i, (src, dst) in enumerate(pairs)]
    for copy in copies:
        copy.start()
    return copies


def first_layer_kernel(
    cuts, owners_hbm, count_hbm, bcount_hbm, x_hbm, wn_hbm, ws_hbm, deg_hbm, brow_hbm, ew_hbm, *rest
):
    near, far = min(2, cuts), cuts - min(2, cuts)
    border_refs, own_refs, slab_refs, local_refs = (
        rest[: far // 2],
        rest[far // 2 : far // 2 + far],
        rest[far // 2 + far : far // 2 + far + near],
        rest[far // 2 + far + near : 2 * far + near],
    )
    rest = rest[2 * far + near :]
    owners_ref, count_ref, bcount_ref, brow_v, deg_v, x_v, wn_v, ws_v, ew_v, pick_v, adj_v, *rest = rest
    scale_v, y_v, sums_v, border_v, sems = rest
    pairs = (
        (brow_hbm, brow_v),
        (owners_hbm, owners_ref),
        (count_hbm, count_ref),
        (bcount_hbm, bcount_ref),
        (deg_hbm, deg_v),
        (ew_hbm, ew_v),
        (x_hbm, x_v),
        (wn_hbm, wn_v),
        (ws_hbm, ws_v),
    )
    brow_in, owners_in, *counts_in, deg_in, ew_in, x_in, wn_in, ws_in = start_all(pairs, sems)
    _, _, neigh, cap, rows = ew_v.shape
    total = cuts * rows
    me = lax.axis_index("cuts")
    lane = lax.broadcasted_iota(jnp.int32, (cap, total), 1)
    eye = (
        lax.broadcasted_iota(jnp.int32, (cap, cap), 0) == lax.broadcasted_iota(jnp.int32, (cap, cap), 1)
    ).astype(F32)
    span = min(cuts, 4)

    def fill_picks(first):
        for k in range(neigh):
            columns = contract_last(eye, brow_v[0, k].astype(F32)).astype(jnp.int32)
            for u in range(span):
                target = columns[:, first + u : first + u + 1] + owners_ref[k, 0, first + u] * rows
                at = u * neigh * cap + k * cap
                pick_v[at : at + cap, :] = (lane == target).astype(F32).astype(BF16)

    brow_in.wait()
    owners_in.wait()
    for first in range(0, cuts, span):
        fill_picks(first)
        if first == 0:
            for copy in (*counts_in, deg_in, ew_in):
                copy.wait()
        for u in range(first, first + span):
            at = slice(u * rows, (u + 1) * rows)
            picks = pick_v[(u - first) * neigh * cap : (u - first + 1) * neigh * cap, :]
            adj_v[at, :] = contract_first(live_tile(ew_v[0, u], count_ref, bcount_ref, u), picks).astype(BF16)
            scale_v[at, :] = as_column(1.0 / deg_v[:, at].astype(F32))
    x_in.wait()
    wn_in.wait()
    for first in range(0, cuts, span):
        at = slice(first * rows, (first + span) * rows)
        y_v[at, :] = jnp.dot(x_v[at, :], wn_v[...], preferred_element_type=F32).astype(BF16)
    ws_in.wait()
    for first in range(0, cuts, span):
        at = slice(first * rows, (first + span) * rows)
        selfs = jnp.dot(x_v[at, :], ws_v[...], preferred_element_type=F32)
        summed = jnp.dot(adj_v[at, :], y_v[...], preferred_element_type=F32)
        sums_v[at, :] = (selfs + summed * scale_v[at, :]).astype(BF16)
    for first in range(0, cuts, span):
        if span < cuts:
            fill_picks(first)
        at = slice(first * neigh * cap, (first + span) * neigh * cap)
        border_v[at, :] = jnp.dot(pick_v[...], sums_v[...], preferred_element_type=F32).astype(BF16)
    direct = direct_rows(rows)
    border = neigh * cap

    def own_at(owner, first, size):
        return pl.ds(pl.multiple_of(owner * rows + first, 16), size)

    def paired_part(out_ref, owner):
        out_ref[: rows - direct, :] = sums_v[own_at(owner, direct, rows - direct), :]
        out_ref[rows - direct :, :] = border_v[pl.ds(pl.multiple_of(owner * border, border), border), :]

    for i, out_ref in enumerate(border_refs):
        paired_part(out_ref, me ^ (2 * i + 3))
    for i, out_ref in enumerate(own_refs):
        out_ref[...] = sums_v[own_at(me ^ (i + 2), 0, direct), :]
    for step, out_ref in enumerate(slab_refs):
        out_ref[:direct, :] = sums_v[own_at(me ^ step, 0, direct), :]
        paired_part(out_ref.at[pl.ds(direct, rows - direct + border)], me ^ step)
    for i, out_ref in enumerate(local_refs):
        paired_part(out_ref, me ^ (2 * i + 2))


def hidden_rows(parts, b1_ref):
    total = parts[0].astype(F32)
    for part in parts[1:]:
        total = total + part.astype(F32)
    return jnp.maximum(total + b1_ref[...], 0.0).astype(BF16)


def prepare_kernel(cuts, reps, subs, after_ref, *rest):
    count_hbm, bcount_hbm, ws_hbm, wn_hbm, b1_hbm, b2_hbm, deg_hbm, ew_hbm, id_hbm = rest[:9]
    w_ref, b1_ref, b2_ref, live_ref, scale_ref, chosen_ref, slots_ref = rest[9:16]
    count_ref, bcount_ref, deg_v, ew_v, id_v, sems = rest[16:]
    units = ws_hbm.shape[0]
    rows = ew_v.shape[2]
    me = lax.axis_index("cuts")
    pairs = (
        (count_hbm, count_ref),
        (bcount_hbm, bcount_ref),
        (deg_hbm, deg_v),
        (id_hbm, id_v),
        (ew_hbm.at[0, me], ew_v),
        (b1_hbm, b1_ref),
        (b2_hbm, b2_ref),
        (ws_hbm, w_ref.at[pl.ds(0, units)]),
        (wn_hbm, w_ref.at[pl.ds(units, units)]),
    )
    copies = start_all(pairs, sems)
    for copy in copies[:5]:
        copy.wait()
    live_ref[...] = live_tile(ew_v[...], count_ref, bcount_ref, me)
    degrees = deg_v[:, pl.ds(pl.multiple_of(me * rows, rows), rows)].astype(F32)
    scale_ref[...] = jnp.broadcast_to(as_column(1.0 / degrees), (rows, rows))
    ids = id_v[...]
    device = ids // rows
    peer = (device // (reps * subs)) * reps + (device // subs) % reps
    slot = (ids - device * rows).astype(F32)
    peer_f = peer.astype(F32)
    down = lax.broadcasted_iota(jnp.int32, (rows, rows), 0)
    across = lax.broadcasted_iota(jnp.int32, (rows, rows), 1)
    earlier = (as_column(peer_f) == peer_f) & (down < across)
    rank = jnp.sum(earlier.astype(F32), axis=0, keepdims=True).astype(jnp.int32)
    place = peer * (rows // (cuts * reps)) + rank
    chosen = down == place
    chosen_ref[...] = chosen.astype(F32).astype(BF16)
    slots = jnp.sum(jnp.where(chosen, slot, 0.0), axis=1, keepdims=True)
    slots_ref[...] = jnp.broadcast_to(slots, (rows, rows)).astype(BF16)
    for copy in copies[5:]:
        copy.wait()


def second_layer_kernel(cuts, *rest):
    near, far = min(2, cuts), cuts - min(2, cuts)
    slab_refs, own_refs, border_refs = rest[:near], rest[near : near + far], rest[near + far : near + far + far // 2]
    w_ref, b1_ref, b2_ref, live_ref, scale_ref, chosen_ref, slots_ref, out_ref = rest[near + far + far // 2 :]
    rows = chosen_ref.shape[0]
    units = w_ref.shape[1]
    direct = direct_rows(rows)
    first = hidden_rows([slab[:direct, :] for slab in slab_refs] + [part[...] for part in own_refs], b1_ref)
    others = hidden_rows([slab[direct:, :] for slab in slab_refs] + [part[...] for part in border_refs], b1_ref)
    own = jnp.concatenate([first, others[: rows - direct]], axis=0)
    border = others[rows - direct :]
    summed = contract_first(live_ref[...], border)
    mean = (summed * scale_ref[:, :1]).astype(BF16)
    z = jnp.dot(jnp.concatenate([own, mean], axis=1), w_ref[...], preferred_element_type=F32) + b2_ref[...]
    scale = lax.rsqrt(jnp.mean(z * z, axis=1, keepdims=True) + 1e-05)
    normalized = (z * scale).astype(BF16)
    out_ref[:, :units] = jnp.dot(chosen_ref[...], normalized, preferred_element_type=F32).astype(BF16)
    out_ref[:, units:] = slots_ref[...]


def placing_kernel(in_ref, out_ref):
    rows, units = out_ref.shape
    across = lax.broadcasted_iota(jnp.int32, (rows, rows), 1)
    chosen = in_ref[:, units:].astype(F32).astype(jnp.int32) == across
    out_ref[...] = contract_first(chosen.astype(F32).astype(BF16), in_ref[:, :units]).astype(BF16)


def body(
    features,
    w_self1,
    w_neigh1,
    bias1,
    w_self2,
    w_neigh2,
    bias2,
    degree,
    neighbor_owners,
    neighbor_count,
    boundary_rows,
    boundary_count,
    edge_weight,
    node_id,
):
    cuts, reps, subs = (lax.axis_size(a) for a in ("cuts", "rep", "sub"))
    total, width = features.shape
    units = w_self1.shape[1]
    _, _, neigh, cap, rows = edge_weight.shape
    border = neigh * cap
    vmem = pl.BlockSpec(memory_space=VMEM)
    hbm = pl.BlockSpec(memory_space=pltpu.HBM)
    shape = jax.ShapeDtypeStruct
    slab = shape((rows + border, units), BF16)
    direct = direct_rows(rows)
    own_slab, border_slab = shape((direct, units), BF16), shape((rows - direct + border, units), BF16)
    near, far = min(2, cuts), cuts - min(2, cuts)
    owners = neighbor_owners.transpose(2, 0, 1)
    bcounts = boundary_count.transpose(2, 0, 1)
    brows = boundary_rows.transpose(0, 2, 1, 3)
    counts_held = [SMEM(a.shape, jnp.int32) for a in (owners, neighbor_count, bcounts)]
    held = total * width + 2 * width * units + total * total + 2 * total * units + 256 * total
    held += min(cuts, 4) * border * total + cuts * border * (units + rows) + units * (near * (rows + border) + far * (rows + border))
    sent = pl.pallas_call(
        functools.partial(first_layer_kernel, cuts),
        out_shape=[border_slab] * (far // 2)
        + [own_slab] * far
        + [slab] * near
        + [border_slab] * (far // 2),
        in_specs=[hbm] * 9,
        out_specs=[vmem] * (2 * far + near),
        scratch_shapes=[
            *counts_held,
            pltpu.VMEM(brows.shape, jnp.int32),
            pltpu.VMEM(degree.shape, jnp.int32),
            pltpu.VMEM((total, width), BF16),
            pltpu.VMEM((width, units), BF16),
            pltpu.VMEM((width, units), BF16),
            pltpu.VMEM(edge_weight.shape, BF16),
            pltpu.VMEM((min(cuts, 4) * border, total), BF16),
            pltpu.VMEM((total, total), BF16),
            pltpu.VMEM((total, 1), F32),
            pltpu.VMEM((total, units), BF16),
            pltpu.VMEM((total, units), BF16),
            pltpu.VMEM((cuts * border, units), BF16),
            pltpu.SemaphoreType.DMA((9,)),
        ],
        compiler_params=pltpu.CompilerParams(vmem_limit_bytes=2 * held + (8 << 20)),
        name="first_layer",
    )(*in_hbm(owners, neighbor_count, bcounts, features, w_neigh1, w_self1, degree, brows, edge_weight))
    sent = list(sent)
    pairs, owns, slabs, local = (
        sent[: far // 2],
        sent[far // 2 : far // 2 + far],
        sent[far // 2 + far : far // 2 + far + near],
        sent[far // 2 + far + near :],
    )
    trade = lambda a, step: lax.ppermute(a, "cuts", partner_pairs(step, cuts))
    pairs = [trade(a, 1) for a in pairs]
    owns = [trade(a, i + 2) for i, a in enumerate(owns)]
    slabs = slabs[:1] + [trade(a, 1) for a in slabs[1:]]
    paired = [(a.astype(F32) + b.astype(F32)).astype(BF16) for a, b in zip(local, pairs)]
    borders = [trade(a, 2 * i + 2) for i, a in enumerate(paired)]
    prepared = pl.pallas_call(
        functools.partial(prepare_kernel, cuts, reps, subs),
        out_shape=[
            shape((2 * units, units), BF16),
            shape((1, units), F32),
            shape((1, units), F32),
            shape((border, rows), BF16),
            shape((rows, rows), F32),
            shape((rows, rows), BF16),
            shape((rows, rows), BF16),
        ],
        in_specs=[pl.BlockSpec(memory_space=pl.ANY)] + [hbm] * 9,
        out_specs=[vmem] * 7,
        scratch_shapes=[
            *counts_held[1:],
            pltpu.VMEM(degree.shape, jnp.int32),
            pltpu.VMEM(edge_weight.shape[2:], BF16),
            pltpu.VMEM(node_id.shape, jnp.int32),
            pltpu.SemaphoreType.DMA((9,)),
        ],
        compiler_params=pltpu.CompilerParams(vmem_limit_bytes=24 << 20),
        cost_estimate=pl.CostEstimate(flops=rows * rows * units, bytes_accessed=4 * units * units, transcendentals=0),
        name="prepare",
    )(
        sent[-1],
        *in_hbm(neighbor_count, bcounts, w_self2, w_neigh2, bias1.reshape(1, units), bias2.reshape(1, units)),
        *in_hbm(degree, edge_weight, node_id),
    )
    arrived = slabs + owns + borders
    payload = pl.pallas_call(
        functools.partial(second_layer_kernel, cuts),
        out_shape=shape((rows, units + rows), BF16),
        in_specs=[vmem] * (len(arrived) + 7),
        out_specs=vmem,
        compiler_params=pltpu.CompilerParams(vmem_limit_bytes=24 << 20),
        name="second_layer",
    )(*arrived, *prepared)
    peers = cuts * reps
    moved = lax.all_to_all(
        payload.reshape(peers, rows // peers, units + rows), ("cuts", "rep"), split_axis=0, concat_axis=0, tiled=True
    )
    return pl.pallas_call(
        placing_kernel,
        out_shape=shape((rows, units), BF16),
        in_specs=[vmem],
        out_specs=vmem,
        name="placing",
    )(pltpu.with_memory_space_constraint(moved.reshape(rows, units + rows), pltpu.VMEM))


def solution(mesh):
    block = ("groups", "rep", "sub")
    placed = (
        P(block, "cuts"),
        P("cuts", None),
        P("cuts", None),
        P(),
        P(),
        P(),
        P(),
        P(block, None),
        P(block, None, None),
        P(block, None),
        P(block, None, None, None),
        P(block, None, None),
        P(block, None, None, None, None),
        P(block, "cuts"),
    )
    return jax.shard_map(
        body,
        mesh=mesh,
        in_specs=placed,
        out_specs=P(("groups", "cuts", "rep", "sub"), None),
        check_vma=False,
    )
```

```python
import functools

import jax
import jax.numpy as jnp
from jax import lax
from jax.experimental import pallas as pl
from jax.experimental.pallas import tpu as pltpu
from jax.sharding import PartitionSpec as P

F32 = jnp.float32
BF16 = jnp.bfloat16
VMEM = pltpu.VMEM
SMEM = pltpu.SMEM
DIRECT = 80


def direct_rows(rows):
    return rows * DIRECT // 128


def pair_chunks(rows, border):
    direct = direct_rows(rows)
    units = (rows - direct + border) // 16
    pieces = -(-units * 16 // direct)
    ends = [16 * (units * i // pieces) for i in range(pieces + 1)]
    return list(zip(ends[:-1], ends[1:]))


def partner_pairs(step, total):
    return [(i, i ^ step) for i in range(total)]


def as_column(row):
    n = row.shape[1]
    eye = lax.broadcasted_iota(jnp.int32, (n, n), 0) == lax.broadcasted_iota(jnp.int32, (n, n), 1)
    return jnp.sum(jnp.where(eye, jnp.broadcast_to(row, (n, n)), 0.0), axis=1, keepdims=True)


def live_limit(count_ref, bcount_ref, owner, k):
    return jnp.where(k < count_ref[0, owner], bcount_ref[k, 0, owner], 0)


def live_tile(tile, count_ref, bcount_ref, owner):
    neigh, cap, rows = tile.shape
    slot = lax.broadcasted_iota(jnp.int32, (cap, rows), 0)
    tiles = []
    for k in range(neigh):
        live = slot < live_limit(count_ref, bcount_ref, owner, k)
        tiles.append(jnp.where(live, tile[k].astype(F32), 0.0).astype(BF16))
    return jnp.concatenate(tiles, axis=0)


def contract_first(a, b):
    return lax.dot_general(a, b, (((0,), (0,)), ((), ())), preferred_element_type=F32)


def contract_last(a, b):
    return lax.dot_general(a, b, (((1,), (1,)), ((), ())), preferred_element_type=F32)


def in_hbm(*arrays):
    return [pltpu.with_memory_space_constraint(a, pltpu.HBM) for a in arrays]


def start_all(pairs, sems):
    copies = [pltpu.make_async_copy(src, dst, sems.at[i]) for i, (src, dst) in enumerate(pairs)]
    for copy in copies:
        copy.start()
    return copies


def first_layer_kernel(
    cuts, owners_hbm, count_hbm, bcount_hbm, x_hbm, wn_hbm, ws_hbm, deg_hbm, brow_hbm, ew_hbm, *rest
):
    near, far = min(2, cuts), cuts - min(2, cuts)
    border_refs, own_refs, slab_refs, local_refs = (
        rest[: far // 2],
        rest[far // 2 : far // 2 + far],
        rest[far // 2 + far : far // 2 + far + near],
        rest[far // 2 + far + near : 2 * far + near],
    )
    rest = rest[2 * far + near :]
    owners_ref, count_ref, bcount_ref, brow_v, deg_v, x_v, wn_v, ws_v, ew_v, pick_v, adj_v, *rest = rest
    scale_v, y_v, sums_v, border_v, sems = rest
    pairs = (
        (brow_hbm, brow_v),
        (owners_hbm, owners_ref),
        (count_hbm, count_ref),
        (bcount_hbm, bcount_ref),
        (deg_hbm, deg_v),
        (ew_hbm, ew_v),
        (x_hbm, x_v),
        (wn_hbm, wn_v),
        (ws_hbm, ws_v),
    )
    brow_in, owners_in, *counts_in, deg_in, ew_in, x_in, wn_in, ws_in = start_all(pairs, sems)
    _, _, neigh, cap, rows = ew_v.shape
    total = cuts * rows
    me = lax.axis_index("cuts")
    lane = lax.broadcasted_iota(jnp.int32, (cap, total), 1)
    eye = (
        lax.broadcasted_iota(jnp.int32, (cap, cap), 0) == lax.broadcasted_iota(jnp.int32, (cap, cap), 1)
    ).astype(F32)
    span = min(cuts, 4)

    def fill_picks(first):
        for k in range(neigh):
            columns = contract_last(eye, brow_v[0, k].astype(F32)).astype(jnp.int32)
            for u in range(span):
                target = columns[:, first + u : first + u + 1] + owners_ref[k, 0, first + u] * rows
                at = u * neigh * cap + k * cap
                pick_v[at : at + cap, :] = (lane == target).astype(F32).astype(BF16)

    brow_in.wait()
    owners_in.wait()
    for first in range(0, cuts, span):
        fill_picks(first)
        if first == 0:
            for copy in (*counts_in, deg_in, ew_in):
                copy.wait()
        for u in range(first, first + span):
            at = slice(u * rows, (u + 1) * rows)
            picks = pick_v[(u - first) * neigh * cap : (u - first + 1) * neigh * cap, :]
            adj_v[at, :] = contract_first(live_tile(ew_v[0, u], count_ref, bcount_ref, u), picks).astype(BF16)
            scale_v[at, :] = as_column(1.0 / deg_v[:, at].astype(F32))
    x_in.wait()
    wn_in.wait()
    for first in range(0, cuts, span):
        at = slice(first * rows, (first + span) * rows)
        y_v[at, :] = jnp.dot(x_v[at, :], wn_v[...], preferred_element_type=F32).astype(BF16)
    ws_in.wait()
    for first in range(0, cuts, span):
        at = slice(first * rows, (first + span) * rows)
        selfs = jnp.dot(x_v[at, :], ws_v[...], preferred_element_type=F32)
        summed = jnp.dot(adj_v[at, :], y_v[...], preferred_element_type=F32)
        sums_v[at, :] = (selfs + summed * scale_v[at, :]).astype(BF16)
    for first in range(0, cuts, span):
        if span < cuts:
            fill_picks(first)
        at = slice(first * neigh * cap, (first + span) * neigh * cap)
        border_v[at, :] = jnp.dot(pick_v[...], sums_v[...], preferred_element_type=F32).astype(BF16)
    direct = direct_rows(rows)
    border = neigh * cap

    def own_at(owner, first, size):
        return pl.ds(pl.multiple_of(owner * rows + first, 16), size)

    def paired_part(out_ref, owner):
        out_ref[: rows - direct, :] = sums_v[own_at(owner, direct, rows - direct), :]
        out_ref[rows - direct :, :] = border_v[pl.ds(pl.multiple_of(owner * border, border), border), :]

    for i, out_ref in enumerate(border_refs):
        paired_part(out_ref, me ^ (2 * i + 3))
    for i, out_ref in enumerate(own_refs):
        out_ref[...] = sums_v[own_at(me ^ (i + 2), 0, direct), :]
    for step, out_ref in enumerate(slab_refs):
        out_ref[:direct, :] = sums_v[own_at(me ^ step, 0, direct), :]
        paired_part(out_ref.at[pl.ds(direct, rows - direct + border)], me ^ step)
    for i, out_ref in enumerate(local_refs):
        paired_part(out_ref, me ^ (2 * i + 2))


def hidden_rows(parts, b1_ref):
    total = parts[0].astype(F32)
    for part in parts[1:]:
        total = total + part.astype(F32)
    return jnp.maximum(total + b1_ref[...], 0.0).astype(BF16)


def prepare_kernel(cuts, reps, subs, after_ref, *rest):
    count_hbm, bcount_hbm, ws_hbm, wn_hbm, b1_hbm, b2_hbm, deg_hbm, ew_hbm, id_hbm = rest[:9]
    w_ref, b1_ref, b2_ref, live_ref, scale_ref, chosen_ref, slots_ref = rest[9:16]
    count_ref, bcount_ref, deg_v, ew_v, id_v, sems = rest[16:]
    units = ws_hbm.shape[0]
    rows = ew_v.shape[2]
    me = lax.axis_index("cuts")
    pairs = (
        (count_hbm, count_ref),
        (bcount_hbm, bcount_ref),
        (deg_hbm, deg_v),
        (id_hbm, id_v),
        (ew_hbm.at[0, me], ew_v),
        (b1_hbm, b1_ref),
        (b2_hbm, b2_ref),
        (ws_hbm, w_ref.at[pl.ds(0, units)]),
        (wn_hbm, w_ref.at[pl.ds(units, units)]),
    )
    copies = start_all(pairs, sems)
    for copy in copies[:5]:
        copy.wait()
    live_ref[...] = live_tile(ew_v[...], count_ref, bcount_ref, me)
    degrees = deg_v[:, pl.ds(pl.multiple_of(me * rows, rows), rows)].astype(F32)
    scale_ref[...] = jnp.broadcast_to(as_column(1.0 / degrees), (rows, rows))
    ids = id_v[...]
    device = ids // rows
    peer = (device // (reps * subs)) * reps + (device // subs) % reps
    slot = (ids - device * rows).astype(F32)
    peer_f = peer.astype(F32)
    down = lax.broadcasted_iota(jnp.int32, (rows, rows), 0)
    across = lax.broadcasted_iota(jnp.int32, (rows, rows), 1)
    earlier = (as_column(peer_f) == peer_f) & (down < across)
    rank = jnp.sum(earlier.astype(F32), axis=0, keepdims=True).astype(jnp.int32)
    place = peer * (rows // (cuts * reps)) + rank
    chosen = down == place
    chosen_ref[...] = chosen.astype(F32).astype(BF16)
    slots = jnp.sum(jnp.where(chosen, slot, 0.0), axis=1, keepdims=True)
    slots_ref[...] = jnp.broadcast_to(slots, (rows, rows)).astype(BF16)
    for copy in copies[5:]:
        copy.wait()


def second_layer_kernel(cuts, *rest):
    near, far = min(2, cuts), cuts - min(2, cuts)
    slab_refs, own_refs, border_refs = rest[:near], rest[near : near + far], rest[near + far : -8]
    w_ref, b1_ref, b2_ref, live_ref, scale_ref, chosen_ref, slots_ref, out_ref = rest[-8:]
    rows = chosen_ref.shape[0]
    chunks = pair_chunks(rows, live_ref.shape[0])
    units = w_ref.shape[1]
    direct = direct_rows(rows)
    first = hidden_rows([slab[:direct, :] for slab in slab_refs] + [part[...] for part in own_refs], b1_ref)
    pieces = []
    for i, (low, high) in enumerate(chunks):
        parts = [slab[direct + low : direct + high, :] for slab in slab_refs]
        pieces.append(hidden_rows(parts + [part[...] for part in border_refs[i :: len(chunks)]], b1_ref))
    others = jnp.concatenate(pieces, axis=0)
    own = jnp.concatenate([first, others[: rows - direct]], axis=0)
    border = others[rows - direct :]
    summed = contract_first(live_ref[...], border)
    mean = (summed * scale_ref[:, :1]).astype(BF16)
    z = jnp.dot(jnp.concatenate([own, mean], axis=1), w_ref[...], preferred_element_type=F32) + b2_ref[...]
    scale = lax.rsqrt(jnp.mean(z * z, axis=1, keepdims=True) + 1e-05)
    normalized = (z * scale).astype(BF16)
    out_ref[:, :units] = jnp.dot(chosen_ref[...], normalized, preferred_element_type=F32).astype(BF16)
    out_ref[:, units:] = slots_ref[...]


def placing_kernel(in_ref, out_ref):
    rows, units = out_ref.shape
    across = lax.broadcasted_iota(jnp.int32, (rows, rows), 1)
    chosen = in_ref[:, units:].astype(F32).astype(jnp.int32) == across
    out_ref[...] = contract_first(chosen.astype(F32).astype(BF16), in_ref[:, :units]).astype(BF16)


def body(
    features,
    w_self1,
    w_neigh1,
    bias1,
    w_self2,
    w_neigh2,
    bias2,
    degree,
    neighbor_owners,
    neighbor_count,
    boundary_rows,
    boundary_count,
    edge_weight,
    node_id,
):
    cuts, reps, subs = (lax.axis_size(a) for a in ("cuts", "rep", "sub"))
    total, width = features.shape
    units = w_self1.shape[1]
    _, _, neigh, cap, rows = edge_weight.shape
    border = neigh * cap
    vmem = pl.BlockSpec(memory_space=VMEM)
    hbm = pl.BlockSpec(memory_space=pltpu.HBM)
    shape = jax.ShapeDtypeStruct
    slab = shape((rows + border, units), BF16)
    direct = direct_rows(rows)
    own_slab, border_slab = shape((direct, units), BF16), shape((rows - direct + border, units), BF16)
    near, far = min(2, cuts), cuts - min(2, cuts)
    owners = neighbor_owners.transpose(2, 0, 1)
    bcounts = boundary_count.transpose(2, 0, 1)
    brows = boundary_rows.transpose(0, 2, 1, 3)
    counts_held = [SMEM(a.shape, jnp.int32) for a in (owners, neighbor_count, bcounts)]
    held = total * width + 2 * width * units + total * total + 2 * total * units + 256 * total
    held += min(cuts, 4) * border * total + cuts * border * (units + rows) + units * (near * (rows + border) + far * (rows + border))
    sent = pl.pallas_call(
        functools.partial(first_layer_kernel, cuts),
        out_shape=[border_slab] * (far // 2)
        + [own_slab] * far
        + [slab] * near
        + [border_slab] * (far // 2),
        in_specs=[hbm] * 9,
        out_specs=[vmem] * (2 * far + near),
        scratch_shapes=[
            *counts_held,
            pltpu.VMEM(brows.shape, jnp.int32),
            pltpu.VMEM(degree.shape, jnp.int32),
            pltpu.VMEM((total, width), BF16),
            pltpu.VMEM((width, units), BF16),
            pltpu.VMEM((width, units), BF16),
            pltpu.VMEM(edge_weight.shape, BF16),
            pltpu.VMEM((min(cuts, 4) * border, total), BF16),
            pltpu.VMEM((total, total), BF16),
            pltpu.VMEM((total, 1), F32),
            pltpu.VMEM((total, units), BF16),
            pltpu.VMEM((total, units), BF16),
            pltpu.VMEM((cuts * border, units), BF16),
            pltpu.SemaphoreType.DMA((9,)),
        ],
        compiler_params=pltpu.CompilerParams(vmem_limit_bytes=2 * held + (8 << 20)),
        name="first_layer",
    )(*in_hbm(owners, neighbor_count, bcounts, features, w_neigh1, w_self1, degree, brows, edge_weight))
    sent = list(sent)
    pairs, owns, slabs, local = (
        sent[: far // 2],
        sent[far // 2 : far // 2 + far],
        sent[far // 2 + far : far // 2 + far + near],
        sent[far // 2 + far + near :],
    )
    trade = lambda a, step: lax.ppermute(a, "cuts", partner_pairs(step, cuts))
    pairs = [trade(a, 1) for a in pairs]
    owns = [trade(a, i + 2) for i, a in enumerate(owns)]
    pairs, waiting = lax.optimization_barrier((pairs, slabs[1:]))
    slabs = slabs[:1] + [trade(a, 1) for a in waiting]
    paired = [(a.astype(F32) + b.astype(F32)).astype(BF16) for a, b in zip(local, pairs)]
    cuts_of = pair_chunks(rows, border)
    borders = [trade(a[low:high], 2 * i + 2) for i, a in enumerate(paired) for low, high in cuts_of]
    prepared = pl.pallas_call(
        functools.partial(prepare_kernel, cuts, reps, subs),
        out_shape=[
            shape((2 * units, units), BF16),
            shape((1, units), F32),
            shape((1, units), F32),
            shape((border, rows), BF16),
            shape((rows, rows), F32),
            shape((rows, rows), BF16),
            shape((rows, rows), BF16),
        ],
        in_specs=[pl.BlockSpec(memory_space=pl.ANY)] + [hbm] * 9,
        out_specs=[vmem] * 7,
        scratch_shapes=[
            *counts_held[1:],
            pltpu.VMEM(degree.shape, jnp.int32),
            pltpu.VMEM(edge_weight.shape[2:], BF16),
            pltpu.VMEM(node_id.shape, jnp.int32),
            pltpu.SemaphoreType.DMA((9,)),
        ],
        compiler_params=pltpu.CompilerParams(vmem_limit_bytes=24 << 20),
        cost_estimate=pl.CostEstimate(flops=rows * rows * units, bytes_accessed=4 * units * units, transcendentals=0),
        name="prepare",
    )(
        sent[-1],
        *in_hbm(neighbor_count, bcounts, w_self2, w_neigh2, bias1.reshape(1, units), bias2.reshape(1, units)),
        *in_hbm(degree, edge_weight, node_id),
    )
    arrived = slabs + owns + borders
    payload = pl.pallas_call(
        functools.partial(second_layer_kernel, cuts),
        out_shape=shape((rows, units + rows), BF16),
        in_specs=[vmem] * (len(arrived) + 7),
        out_specs=vmem,
        compiler_params=pltpu.CompilerParams(vmem_limit_bytes=24 << 20),
        name="second_layer",
    )(*arrived, *prepared)
    peers = cuts * reps
    moved = lax.all_to_all(
        payload.reshape(peers, rows // peers, units + rows), ("cuts", "rep"), split_axis=0, concat_axis=0, tiled=True
    )
    return pl.pallas_call(
        placing_kernel,
        out_shape=shape((rows, units), BF16),
        in_specs=[vmem],
        out_specs=vmem,
        name="placing",
    )(pltpu.with_memory_space_constraint(moved.reshape(rows, units + rows), pltpu.VMEM))


def solution(mesh):
    block = ("groups", "rep", "sub")
    placed = (
        P(block, "cuts"),
        P("cuts", None),
        P("cuts", None),
        P(),
        P(),
        P(),
        P(),
        P(block, None),
        P(block, None, None),
        P(block, None),
        P(block, None, None, None),
        P(block, None, None),
        P(block, None, None, None, None),
        P(block, "cuts"),
    )
    return jax.shard_map(
        body,
        mesh=mesh,
        in_specs=placed,
        out_specs=P(("groups", "cuts", "rep", "sub"), None),
        check_vma=False,
    )
```

```python
import functools

import jax
import jax.numpy as jnp
from jax import lax
from jax.experimental import pallas as pl
from jax.experimental.pallas import tpu as pltpu
from jax.sharding import PartitionSpec as P

F32 = jnp.float32
BF16 = jnp.bfloat16
VMEM = pltpu.VMEM
SMEM = pltpu.SMEM


def pair_chunks(rows, border):
    pieces = -(-rows // border)
    ends = [rows * i // pieces // 16 * 16 for i in range(pieces)] + [rows]
    return list(zip(ends[:-1], ends[1:]))


def partner_pairs(step, total):
    return [(i, i ^ step) for i in range(total)]


def as_column(row):
    n = row.shape[1]
    eye = lax.broadcasted_iota(jnp.int32, (n, n), 0) == lax.broadcasted_iota(jnp.int32, (n, n), 1)
    return jnp.sum(jnp.where(eye, jnp.broadcast_to(row, (n, n)), 0.0), axis=1, keepdims=True)


def live_limit(count_ref, bcount_ref, owner, k):
    return jnp.where(k < count_ref[0, owner], bcount_ref[k, 0, owner], 0)


def live_tile(tile, count_ref, bcount_ref, owner):
    neigh, cap, rows = tile.shape
    slot = lax.broadcasted_iota(jnp.int32, (cap, rows), 0)
    tiles = []
    for k in range(neigh):
        live = slot < live_limit(count_ref, bcount_ref, owner, k)
        tiles.append(jnp.where(live, tile[k].astype(F32), 0.0).astype(BF16))
    return jnp.concatenate(tiles, axis=0)


def contract_first(a, b):
    return lax.dot_general(a, b, (((0,), (0,)), ((), ())), preferred_element_type=F32)


def contract_last(a, b):
    return lax.dot_general(a, b, (((1,), (1,)), ((), ())), preferred_element_type=F32)


def in_hbm(*arrays):
    return [pltpu.with_memory_space_constraint(a, pltpu.HBM) for a in arrays]


def start_all(pairs, sems):
    copies = [pltpu.make_async_copy(src, dst, sems.at[i]) for i, (src, dst) in enumerate(pairs)]
    for copy in copies:
        copy.start()
    return copies


def fill_picks(pick_ref, brow_ref, owners_ref, first, rows):
    _, neigh, _, cap = brow_ref.shape
    total = pick_ref.shape[1]
    lane = lax.broadcasted_iota(jnp.int32, (cap, total), 1)
    eye = (
        lax.broadcasted_iota(jnp.int32, (cap, cap), 0) == lax.broadcasted_iota(jnp.int32, (cap, cap), 1)
    ).astype(F32)
    for k in range(neigh):
        columns = contract_last(eye, brow_ref[0, k].astype(F32)).astype(jnp.int32)
        for u in range(pick_ref.shape[0] // (neigh * cap)):
            target = columns[:, first + u : first + u + 1] + owners_ref[k, 0, first + u] * rows
            at = u * neigh * cap + k * cap
            pick_ref[at : at + cap, :] = (lane == target).astype(F32).astype(BF16)


def first_layer_kernel(
    cuts, owners_hbm, count_hbm, bcount_hbm, x_hbm, wn_hbm, ws_hbm, deg_hbm, brow_hbm, ew_hbm, *rest
):
    far = cuts - min(2, cuts)
    own_refs, sums_ref, pick_ref, rest = rest[:far], rest[far], rest[far + 1], rest[far + 2 :]
    owners_ref, count_ref, bcount_ref, brow_v, deg_v, x_v, wn_v, ws_v, ew_v, adj_v, scale_v, y_v, sems = rest
    pairs = (
        (brow_hbm, brow_v),
        (owners_hbm, owners_ref),
        (count_hbm, count_ref),
        (bcount_hbm, bcount_ref),
        (deg_hbm, deg_v),
        (ew_hbm, ew_v),
        (x_hbm, x_v),
        (wn_hbm, wn_v),
        (ws_hbm, ws_v),
    )
    brow_in, owners_in, *counts_in, deg_in, ew_in, x_in, wn_in, ws_in = start_all(pairs, sems)
    _, _, neigh, cap, rows = ew_v.shape
    me = lax.axis_index("cuts")
    span = min(cuts, 4)
    brow_in.wait()
    owners_in.wait()
    for first in range(0, cuts, span):
        fill_picks(pick_ref, brow_v, owners_ref, first, rows)
        if first == 0:
            for copy in (*counts_in, deg_in, ew_in):
                copy.wait()
        for u in range(first, first + span):
            at = slice(u * rows, (u + 1) * rows)
            picks = pick_ref[(u - first) * neigh * cap : (u - first + 1) * neigh * cap, :]
            adj_v[at, :] = contract_first(live_tile(ew_v[0, u], count_ref, bcount_ref, u), picks).astype(BF16)
            scale_v[at, :] = as_column(1.0 / deg_v[:, at].astype(F32))
    x_in.wait()
    wn_in.wait()
    for first in range(0, cuts, span):
        at = slice(first * rows, (first + span) * rows)
        y_v[at, :] = jnp.dot(x_v[at, :], wn_v[...], preferred_element_type=F32).astype(BF16)
    ws_in.wait()
    for first in range(0, cuts, span):
        at = slice(first * rows, (first + span) * rows)
        selfs = jnp.dot(x_v[at, :], ws_v[...], preferred_element_type=F32)
        summed = jnp.dot(adj_v[at, :], y_v[...], preferred_element_type=F32)
        sums_ref[at, :] = (selfs + summed * scale_v[at, :]).astype(BF16)
    for i, out_ref in enumerate(own_refs):
        out_ref[...] = sums_ref[pl.ds(pl.multiple_of((me ^ (i + 2)) * rows, rows), rows), :]


def border_kernel(cuts, rows, cap, sums_ref, pick_ref, *rest):
    near, far = min(2, cuts), cuts - min(2, cuts)
    span = min(cuts, 4)
    border = pick_ref.shape[0] // span
    if span < cuts:
        brow_hbm, owners_hbm, *rest = rest
        brow_v, owners_v, pick_v, sems = rest[-4:]
        for copy in start_all(((brow_hbm, brow_v), (owners_hbm, owners_v)), sems):
            copy.wait()
    far_refs, slab_refs, border_v = rest[:far], rest[far : far + near], rest[far + near]
    me = lax.axis_index("cuts")
    for first in range(0, cuts, span):
        if span < cuts:
            fill_picks(pick_v, brow_v, owners_v, first, rows)
        picks = pick_ref if span == cuts else pick_v
        at = slice(first * border, (first + span) * border)
        border_v[at, :] = jnp.dot(picks[...], sums_ref[...], preferred_element_type=F32).astype(BF16)

    def border_of(owner):
        return border_v[pl.ds(pl.multiple_of(owner * border, border), border), :]

    for i, out_ref in enumerate(far_refs):
        out_ref[...] = border_of(me ^ (i + 2))
    for step, out_ref in enumerate(slab_refs):
        out_ref[:rows, :] = sums_ref[pl.ds(pl.multiple_of((me ^ step) * rows, rows), rows), :]
        out_ref[rows:, :] = border_of(me ^ step)


def hidden_rows(parts, b1_ref):
    total = parts[0].astype(F32)
    for part in parts[1:]:
        total = total + part.astype(F32)
    return jnp.maximum(total + b1_ref[...], 0.0).astype(BF16)


def prepare_kernel(cuts, reps, subs, after_ref, *rest):
    count_hbm, bcount_hbm, ws_hbm, wn_hbm, b1_hbm, b2_hbm, deg_hbm, ew_hbm, id_hbm = rest[:9]
    w_ref, b1_ref, b2_ref, live_ref, scale_ref, chosen_ref, slots_ref = rest[9:16]
    count_ref, bcount_ref, deg_v, ew_v, id_v, sems = rest[16:]
    units = ws_hbm.shape[0]
    rows = ew_v.shape[2]
    me = lax.axis_index("cuts")
    pairs = (
        (count_hbm, count_ref),
        (bcount_hbm, bcount_ref),
        (deg_hbm, deg_v),
        (id_hbm, id_v),
        (ew_hbm.at[0, me], ew_v),
        (b1_hbm, b1_ref),
        (b2_hbm, b2_ref),
        (ws_hbm, w_ref.at[pl.ds(0, units)]),
        (wn_hbm, w_ref.at[pl.ds(units, units)]),
    )
    copies = start_all(pairs, sems)
    for copy in copies[:5]:
        copy.wait()
    live_ref[...] = live_tile(ew_v[...], count_ref, bcount_ref, me)
    degrees = deg_v[:, pl.ds(pl.multiple_of(me * rows, rows), rows)].astype(F32)
    scale_ref[...] = jnp.broadcast_to(as_column(1.0 / degrees), (rows, rows))
    ids = id_v[...]
    device = ids // rows
    peer = (device // (reps * subs)) * reps + (device // subs) % reps
    slot = (ids - device * rows).astype(F32)
    peer_f = peer.astype(F32)
    down = lax.broadcasted_iota(jnp.int32, (rows, rows), 0)
    across = lax.broadcasted_iota(jnp.int32, (rows, rows), 1)
    earlier = (as_column(peer_f) == peer_f) & (down < across)
    rank = jnp.sum(earlier.astype(F32), axis=0, keepdims=True).astype(jnp.int32)
    place = peer * (rows // (cuts * reps)) + rank
    chosen = down == place
    chosen_ref[...] = chosen.astype(F32).astype(BF16)
    slots = jnp.sum(jnp.where(chosen, slot, 0.0), axis=1, keepdims=True)
    slots_ref[...] = jnp.broadcast_to(slots, (rows, rows)).astype(BF16)
    for copy in copies[5:]:
        copy.wait()


def second_layer_kernel(cuts, *rest):
    near, far = min(2, cuts), cuts - min(2, cuts)
    slab_refs, border_refs, own_refs = rest[:near], rest[near : near + far], rest[near + far : -8]
    w_ref, b1_ref, b2_ref, live_ref, scale_ref, chosen_ref, slots_ref, out_ref = rest[-8:]
    rows = chosen_ref.shape[0]
    units = w_ref.shape[1]
    chunks = pair_chunks(rows, live_ref.shape[0])
    border = hidden_rows([slab[rows:, :] for slab in slab_refs] + [part[...] for part in border_refs], b1_ref)
    pieces = []
    for i, (low, high) in enumerate(chunks):
        parts = [slab[low:high, :] for slab in slab_refs] + [part[...] for part in own_refs[i :: len(chunks)]]
        pieces.append(hidden_rows(parts, b1_ref))
    own = jnp.concatenate(pieces, axis=0)
    summed = contract_first(live_ref[...], border)
    mean = (summed * scale_ref[:, :1]).astype(BF16)
    z = jnp.dot(jnp.concatenate([own, mean], axis=1), w_ref[...], preferred_element_type=F32) + b2_ref[...]
    scale = lax.rsqrt(jnp.mean(z * z, axis=1, keepdims=True) + 1e-05)
    normalized = (z * scale).astype(BF16)
    out_ref[:, :units] = jnp.dot(chosen_ref[...], normalized, preferred_element_type=F32).astype(BF16)
    out_ref[:, units:] = slots_ref[...]


def placing_kernel(in_ref, out_ref):
    rows, units = out_ref.shape
    across = lax.broadcasted_iota(jnp.int32, (rows, rows), 1)
    chosen = in_ref[:, units:].astype(F32).astype(jnp.int32) == across
    out_ref[...] = contract_first(chosen.astype(F32).astype(BF16), in_ref[:, :units]).astype(BF16)


def body(
    features,
    w_self1,
    w_neigh1,
    bias1,
    w_self2,
    w_neigh2,
    bias2,
    degree,
    neighbor_owners,
    neighbor_count,
    boundary_rows,
    boundary_count,
    edge_weight,
    node_id,
):
    cuts, reps, subs = (lax.axis_size(a) for a in ("cuts", "rep", "sub"))
    total, width = features.shape
    units = w_self1.shape[1]
    _, _, neigh, cap, rows = edge_weight.shape
    border = neigh * cap
    vmem = pl.BlockSpec(memory_space=VMEM)
    hbm = pl.BlockSpec(memory_space=pltpu.HBM)
    shape = jax.ShapeDtypeStruct
    slab = shape((rows + border, units), BF16)
    own_slab, border_slab = shape((rows, units), BF16), shape((border, units), BF16)
    near, far = min(2, cuts), cuts - min(2, cuts)
    owners = neighbor_owners.transpose(2, 0, 1)
    bcounts = boundary_count.transpose(2, 0, 1)
    brows = boundary_rows.transpose(0, 2, 1, 3)
    counts_held = [SMEM(a.shape, jnp.int32) for a in (owners, neighbor_count, bcounts)]
    span = min(cuts, 4)
    held = total * width + 2 * width * units + total * total + 2 * total * units + 256 * total
    held += span * border * total + cuts * border * rows + far * rows * units
    *owns, sums, pick = pl.pallas_call(
        functools.partial(first_layer_kernel, cuts),
        out_shape=[own_slab] * far + [shape((total, units), BF16), shape((span * border, total), BF16)],
        in_specs=[hbm] * 9,
        out_specs=[vmem] * (far + 2),
        scratch_shapes=[
            *counts_held,
            pltpu.VMEM(brows.shape, jnp.int32),
            pltpu.VMEM(degree.shape, jnp.int32),
            pltpu.VMEM((total, width), BF16),
            pltpu.VMEM((width, units), BF16),
            pltpu.VMEM((width, units), BF16),
            pltpu.VMEM(edge_weight.shape, BF16),
            pltpu.VMEM((total, total), BF16),
            pltpu.VMEM((total, 1), F32),
            pltpu.VMEM((total, units), BF16),
            pltpu.SemaphoreType.DMA((9,)),
        ],
        compiler_params=pltpu.CompilerParams(vmem_limit_bytes=2 * held + (8 << 20)),
        name="first_layer",
    )(*in_hbm(owners, neighbor_count, bcounts, features, w_neigh1, w_self1, degree, brows, edge_weight))
    rebuilt = span < cuts
    held = total * units + 2 * span * border * total + cuts * border * units + units * cuts * (rows + border)
    *borders, first_slab, second_slab = pl.pallas_call(
        functools.partial(border_kernel, cuts, rows, cap),
        out_shape=[border_slab] * far + [slab] * near,
        in_specs=[vmem] * 2 + [hbm] * (2 * rebuilt),
        out_specs=[vmem] * cuts,
        scratch_shapes=[pltpu.VMEM((cuts * border, units), BF16)]
        + [
            pltpu.VMEM(brows.shape, jnp.int32),
            counts_held[0],
            pltpu.VMEM((span * border, total), BF16),
            pltpu.SemaphoreType.DMA((2,)),
        ]
        * rebuilt,
        compiler_params=pltpu.CompilerParams(vmem_limit_bytes=2 * held + (8 << 20)),
        cost_estimate=pl.CostEstimate(flops=2 * cuts * border * total * units, bytes_accessed=0, transcendentals=0),
        name="border",
    )(sums, pick, *in_hbm(*(brows, owners)[: 2 * rebuilt]))
    trade = lambda a, step: lax.ppermute(a, "cuts", partner_pairs(step, cuts))
    pairs = [trade(a, 1) for a in owns[1::2]]
    pairs, waiting, odd = lax.optimization_barrier((pairs, second_slab, borders[1::2]))
    borders = [trade(odd[i // 2] if i % 2 else a, i + 2) for i, a in enumerate(borders)]
    slabs = [first_slab, trade(waiting, 1)]
    paired = [(a.astype(F32) + b.astype(F32)).astype(BF16) for a, b in zip(owns[::2], pairs)]
    chunks = pair_chunks(rows, border)
    owns = [trade(a[low:high], 2 * i + 2) for i, a in enumerate(paired) for low, high in chunks]
    prepared = pl.pallas_call(
        functools.partial(prepare_kernel, cuts, reps, subs),
        out_shape=[
            shape((2 * units, units), BF16),
            shape((1, units), F32),
            shape((1, units), F32),
            shape((border, rows), BF16),
            shape((rows, rows), F32),
            shape((rows, rows), BF16),
            shape((rows, rows), BF16),
        ],
        in_specs=[pl.BlockSpec(memory_space=pl.ANY)] + [hbm] * 9,
        out_specs=[vmem] * 7,
        scratch_shapes=[
            *counts_held[1:],
            pltpu.VMEM(degree.shape, jnp.int32),
            pltpu.VMEM(edge_weight.shape[2:], BF16),
            pltpu.VMEM(node_id.shape, jnp.int32),
            pltpu.SemaphoreType.DMA((9,)),
        ],
        compiler_params=pltpu.CompilerParams(vmem_limit_bytes=24 << 20),
        cost_estimate=pl.CostEstimate(flops=rows * rows * units, bytes_accessed=4 * units * units, transcendentals=0),
        name="prepare",
    )(
        sums,
        *in_hbm(neighbor_count, bcounts, w_self2, w_neigh2, bias1.reshape(1, units), bias2.reshape(1, units)),
        *in_hbm(degree, edge_weight, node_id),
    )
    arrived = slabs + borders + owns
    payload = pl.pallas_call(
        functools.partial(second_layer_kernel, cuts),
        out_shape=shape((rows, units + rows), BF16),
        in_specs=[vmem] * (len(arrived) + 7),
        out_specs=vmem,
        compiler_params=pltpu.CompilerParams(vmem_limit_bytes=24 << 20),
        name="second_layer",
    )(*arrived, *prepared)
    peers = cuts * reps
    moved = lax.all_to_all(
        payload.reshape(peers, rows // peers, units + rows), ("cuts", "rep"), split_axis=0, concat_axis=0, tiled=True
    )
    return pl.pallas_call(
        placing_kernel,
        out_shape=shape((rows, units), BF16),
        in_specs=[vmem],
        out_specs=vmem,
        name="placing",
    )(pltpu.with_memory_space_constraint(moved.reshape(rows, units + rows), pltpu.VMEM))


def solution(mesh):
    block = ("groups", "rep", "sub")
    placed = (
        P(block, "cuts"),
        P("cuts", None),
        P("cuts", None),
        P(),
        P(),
        P(),
        P(),
        P(block, None),
        P(block, None, None),
        P(block, None),
        P(block, None, None, None),
        P(block, None, None),
        P(block, None, None, None, None),
        P(block, "cuts"),
    )
    return jax.shard_map(
        body,
        mesh=mesh,
        in_specs=placed,
        out_specs=P(("groups", "cuts", "rep", "sub"), None),
        check_vma=False,
    )
```

```python
import functools

import jax
import jax.numpy as jnp
from jax import lax
from jax.experimental import pallas as pl
from jax.experimental.pallas import tpu as pltpu
from jax.sharding import PartitionSpec as P

F32 = jnp.float32
BF16 = jnp.bfloat16
VMEM = pltpu.VMEM
SMEM = pltpu.SMEM
DIRECT = 64
WEIGHT = 20_000_000_000


def direct_rows(rows):
    return rows * DIRECT // 128


def pair_chunks(rows, border):
    direct = direct_rows(rows)
    units = (rows - direct + border) // 16
    pieces = 1
    ends = [16 * (units * i // pieces) for i in range(pieces + 1)]
    return list(zip(ends[:-1], ends[1:]))


def partner_pairs(step, total):
    return [(i, i ^ step) for i in range(total)]


def as_column(row):
    n = row.shape[1]
    eye = lax.broadcasted_iota(jnp.int32, (n, n), 0) == lax.broadcasted_iota(jnp.int32, (n, n), 1)
    return jnp.sum(jnp.where(eye, jnp.broadcast_to(row, (n, n)), 0.0), axis=1, keepdims=True)


def live_limit(count_ref, bcount_ref, owner, k):
    return jnp.where(k < count_ref[0, owner], bcount_ref[k, 0, owner], 0)


def live_tile(tile, count_ref, bcount_ref, owner):
    neigh, cap, rows = tile.shape
    slot = lax.broadcasted_iota(jnp.int32, (cap, rows), 0)
    tiles = []
    for k in range(neigh):
        live = slot < live_limit(count_ref, bcount_ref, owner, k)
        tiles.append(jnp.where(live, tile[k].astype(F32), 0.0).astype(BF16))
    return jnp.concatenate(tiles, axis=0)


def contract_first(a, b):
    return lax.dot_general(a, b, (((0,), (0,)), ((), ())), preferred_element_type=F32)


def contract_last(a, b):
    return lax.dot_general(a, b, (((1,), (1,)), ((), ())), preferred_element_type=F32)


def in_hbm(*arrays):
    return [pltpu.with_memory_space_constraint(a, pltpu.HBM) for a in arrays]


def start_all(pairs, sems):
    copies = [pltpu.make_async_copy(src, dst, sems.at[i]) for i, (src, dst) in enumerate(pairs)]
    for copy in copies:
        copy.start()
    return copies


def first_layer_kernel(
    cuts, owners_hbm, count_hbm, bcount_hbm, x_hbm, wn_hbm, ws_hbm, deg_hbm, brow_hbm, ew_hbm, *rest
):
    near, far = min(2, cuts), cuts - min(2, cuts)
    border_refs, own_refs, slab_refs, local_refs = (
        rest[: far // 2],
        rest[far // 2 : far // 2 + far],
        rest[far // 2 + far : far // 2 + far + near],
        rest[far // 2 + far + near : 2 * far + near],
    )
    rest = rest[2 * far + near :]
    owners_ref, count_ref, bcount_ref, brow_v, deg_v, x_v, wn_v, ws_v, ew_v, pick_v, adj_v, *rest = rest
    scale_v, y_v, sums_v, border_v, sems = rest
    pairs = (
        (brow_hbm, brow_v),
        (owners_hbm, owners_ref),
        (count_hbm, count_ref),
        (bcount_hbm, bcount_ref),
        (deg_hbm, deg_v),
        (ew_hbm, ew_v),
        (x_hbm, x_v),
        (wn_hbm, wn_v),
        (ws_hbm, ws_v),
    )
    brow_in, owners_in, *counts_in, deg_in, ew_in, x_in, wn_in, ws_in = start_all(pairs, sems)
    _, _, neigh, cap, rows = ew_v.shape
    total = cuts * rows
    me = lax.axis_index("cuts")
    lane = lax.broadcasted_iota(jnp.int32, (cap, total), 1)
    eye = (
        lax.broadcasted_iota(jnp.int32, (cap, cap), 0) == lax.broadcasted_iota(jnp.int32, (cap, cap), 1)
    ).astype(F32)
    span = min(cuts, 4)

    def fill_picks(first):
        for k in range(neigh):
            columns = contract_last(eye, brow_v[0, k].astype(F32)).astype(jnp.int32)
            for u in range(span):
                target = columns[:, first + u : first + u + 1] + owners_ref[k, 0, first + u] * rows
                at = u * neigh * cap + k * cap
                pick_v[at : at + cap, :] = (lane == target).astype(F32).astype(BF16)

    brow_in.wait()
    owners_in.wait()
    for first in range(0, cuts, span):
        fill_picks(first)
        if first == 0:
            for copy in (*counts_in, deg_in, ew_in):
                copy.wait()
        for u in range(first, first + span):
            at = slice(u * rows, (u + 1) * rows)
            picks = pick_v[(u - first) * neigh * cap : (u - first + 1) * neigh * cap, :]
            adj_v[at, :] = contract_first(live_tile(ew_v[0, u], count_ref, bcount_ref, u), picks).astype(BF16)
            scale_v[at, :] = as_column(1.0 / deg_v[:, at].astype(F32))
    x_in.wait()
    wn_in.wait()
    for first in range(0, cuts, span):
        at = slice(first * rows, (first + span) * rows)
        y_v[at, :] = jnp.dot(x_v[at, :], wn_v[...], preferred_element_type=F32).astype(BF16)
    ws_in.wait()
    for first in range(0, cuts, span):
        at = slice(first * rows, (first + span) * rows)
        selfs = jnp.dot(x_v[at, :], ws_v[...], preferred_element_type=F32)
        summed = jnp.dot(adj_v[at, :], y_v[...], preferred_element_type=F32)
        sums_v[at, :] = (selfs + summed * scale_v[at, :]).astype(BF16)
    for first in range(0, cuts, span):
        if span < cuts:
            fill_picks(first)
        at = slice(first * neigh * cap, (first + span) * neigh * cap)
        border_v[at, :] = jnp.dot(pick_v[...], sums_v[...], preferred_element_type=F32).astype(BF16)
    direct = direct_rows(rows)
    border = neigh * cap

    def own_at(owner, first, size):
        return pl.ds(pl.multiple_of(owner * rows + first, 16), size)

    def paired_part(out_ref, owner):
        out_ref[: rows - direct, :] = sums_v[own_at(owner, direct, rows - direct), :]
        out_ref[rows - direct :, :] = border_v[pl.ds(pl.multiple_of(owner * border, border), border), :]

    for i, out_ref in enumerate(border_refs):
        paired_part(out_ref, me ^ (2 * i + 3))
    for i, out_ref in enumerate(own_refs):
        out_ref[...] = sums_v[own_at(me ^ (i + 2), 0, direct), :]
    for step, out_ref in enumerate(slab_refs):
        out_ref[:direct, :] = sums_v[own_at(me ^ step, 0, direct), :]
        paired_part(out_ref.at[pl.ds(direct, rows - direct + border)], me ^ step)
    for i, out_ref in enumerate(local_refs):
        paired_part(out_ref, me ^ (2 * i + 2))


def hidden_rows(parts, b1_ref):
    total = parts[0].astype(F32)
    for part in parts[1:]:
        total = total + part.astype(F32)
    return jnp.maximum(total + b1_ref[...], 0.0).astype(BF16)


def prepare_kernel(cuts, reps, subs, after_ref, *rest):
    count_hbm, bcount_hbm, ws_hbm, wn_hbm, b1_hbm, b2_hbm, deg_hbm, ew_hbm, id_hbm = rest[:9]
    w_ref, b1_ref, b2_ref, live_ref, scale_ref, chosen_ref, slots_ref = rest[9:16]
    count_ref, bcount_ref, deg_v, ew_v, id_v, sems = rest[16:]
    units = ws_hbm.shape[0]
    rows = ew_v.shape[2]
    me = lax.axis_index("cuts")
    pairs = (
        (count_hbm, count_ref),
        (bcount_hbm, bcount_ref),
        (deg_hbm, deg_v),
        (id_hbm, id_v),
        (ew_hbm.at[0, me], ew_v),
        (b1_hbm, b1_ref),
        (b2_hbm, b2_ref),
        (ws_hbm, w_ref.at[pl.ds(0, units)]),
        (wn_hbm, w_ref.at[pl.ds(units, units)]),
    )
    copies = start_all(pairs, sems)
    for copy in copies[:5]:
        copy.wait()
    live_ref[...] = live_tile(ew_v[...], count_ref, bcount_ref, me)
    degrees = deg_v[:, pl.ds(pl.multiple_of(me * rows, rows), rows)].astype(F32)
    scale_ref[...] = jnp.broadcast_to(as_column(1.0 / degrees), (rows, rows))
    ids = id_v[...]
    device = ids // rows
    peer = (device // (reps * subs)) * reps + (device // subs) % reps
    slot = (ids - device * rows).astype(F32)
    peer_f = peer.astype(F32)
    down = lax.broadcasted_iota(jnp.int32, (rows, rows), 0)
    across = lax.broadcasted_iota(jnp.int32, (rows, rows), 1)
    earlier = (as_column(peer_f) == peer_f) & (down < across)
    rank = jnp.sum(earlier.astype(F32), axis=0, keepdims=True).astype(jnp.int32)
    place = peer * (rows // (cuts * reps)) + rank
    chosen = down == place
    chosen_ref[...] = chosen.astype(F32).astype(BF16)
    slots = jnp.sum(jnp.where(chosen, slot, 0.0), axis=1, keepdims=True)
    slots_ref[...] = jnp.broadcast_to(slots, (rows, rows)).astype(BF16)
    for copy in copies[5:]:
        copy.wait()


def second_layer_kernel(cuts, *rest):
    near, far = min(2, cuts), cuts - min(2, cuts)
    slab_refs, own_refs, border_refs = rest[:near], rest[near : near + far], rest[near + far : -8]
    w_ref, b1_ref, b2_ref, live_ref, scale_ref, chosen_ref, slots_ref, out_ref = rest[-8:]
    rows = chosen_ref.shape[0]
    chunks = pair_chunks(rows, live_ref.shape[0])
    units = w_ref.shape[1]
    direct = direct_rows(rows)
    first = hidden_rows([slab[:direct, :] for slab in slab_refs] + [part[...] for part in own_refs], b1_ref)
    pieces = []
    for i, (low, high) in enumerate(chunks):
        parts = [slab[direct + low : direct + high, :] for slab in slab_refs]
        pieces.append(hidden_rows(parts + [part[...] for part in border_refs[i :: len(chunks)]], b1_ref))
    others = jnp.concatenate(pieces, axis=0)
    own = jnp.concatenate([first, others[: rows - direct]], axis=0)
    border = others[rows - direct :]
    summed = contract_first(live_ref[...], border)
    mean = (summed * scale_ref[:, :1]).astype(BF16)
    z = jnp.dot(jnp.concatenate([own, mean], axis=1), w_ref[...], preferred_element_type=F32) + b2_ref[...]
    scale = lax.rsqrt(jnp.mean(z * z, axis=1, keepdims=True) + 1e-05)
    normalized = (z * scale).astype(BF16)
    out_ref[:, :units] = jnp.dot(chosen_ref[...], normalized, preferred_element_type=F32).astype(BF16)
    out_ref[:, units:] = slots_ref[...]


def placing_kernel(in_ref, out_ref):
    rows, units = out_ref.shape
    across = lax.broadcasted_iota(jnp.int32, (rows, rows), 1)
    chosen = in_ref[:, units:].astype(F32).astype(jnp.int32) == across
    out_ref[...] = contract_first(chosen.astype(F32).astype(BF16), in_ref[:, :units]).astype(BF16)


def body(
    features,
    w_self1,
    w_neigh1,
    bias1,
    w_self2,
    w_neigh2,
    bias2,
    degree,
    neighbor_owners,
    neighbor_count,
    boundary_rows,
    boundary_count,
    edge_weight,
    node_id,
):
    cuts, reps, subs = (lax.axis_size(a) for a in ("cuts", "rep", "sub"))
    total, width = features.shape
    units = w_self1.shape[1]
    _, _, neigh, cap, rows = edge_weight.shape
    border = neigh * cap
    vmem = pl.BlockSpec(memory_space=VMEM)
    hbm = pl.BlockSpec(memory_space=pltpu.HBM)
    shape = jax.ShapeDtypeStruct
    slab = shape((rows + border, units), BF16)
    direct = direct_rows(rows)
    own_slab, border_slab = shape((direct, units), BF16), shape((rows - direct + border, units), BF16)
    near, far = min(2, cuts), cuts - min(2, cuts)
    owners = neighbor_owners.transpose(2, 0, 1)
    bcounts = boundary_count.transpose(2, 0, 1)
    brows = boundary_rows.transpose(0, 2, 1, 3)
    counts_held = [SMEM(a.shape, jnp.int32) for a in (owners, neighbor_count, bcounts)]
    held = total * width + 2 * width * units + total * total + 2 * total * units + 256 * total
    held += min(cuts, 4) * border * total + cuts * border * (units + rows) + units * (near * (rows + border) + far * (rows + border))
    sent = pl.pallas_call(
        functools.partial(first_layer_kernel, cuts),
        out_shape=[border_slab] * (far // 2)
        + [own_slab] * far
        + [slab] * near
        + [border_slab] * (far // 2),
        in_specs=[hbm] * 9,
        out_specs=[vmem] * (2 * far + near),
        scratch_shapes=[
            *counts_held,
            pltpu.VMEM(brows.shape, jnp.int32),
            pltpu.VMEM(degree.shape, jnp.int32),
            pltpu.VMEM((total, width), BF16),
            pltpu.VMEM((width, units), BF16),
            pltpu.VMEM((width, units), BF16),
            pltpu.VMEM(edge_weight.shape, BF16),
            pltpu.VMEM((min(cuts, 4) * border, total), BF16),
            pltpu.VMEM((total, total), BF16),
            pltpu.VMEM((total, 1), F32),
            pltpu.VMEM((total, units), BF16),
            pltpu.VMEM((total, units), BF16),
            pltpu.VMEM((cuts * border, units), BF16),
            pltpu.SemaphoreType.DMA((9,)),
        ],
        compiler_params=pltpu.CompilerParams(vmem_limit_bytes=2 * held + (8 << 20)),
        name="first_layer",
    )(*in_hbm(owners, neighbor_count, bcounts, features, w_neigh1, w_self1, degree, brows, edge_weight))
    sent = list(sent)
    pairs, owns, slabs, local = (
        sent[: far // 2],
        sent[far // 2 : far // 2 + far],
        sent[far // 2 + far : far // 2 + far + near],
        sent[far // 2 + far + near :],
    )
    trade = lambda a, step: lax.ppermute(a, "cuts", partner_pairs(step, cuts))
    pairs = [trade(a, 1) for a in pairs]
    owns = [trade(a, i + 2) for i, a in enumerate(owns)]
    pairs, waiting = lax.optimization_barrier((pairs, slabs[1:]))
    slabs = slabs[:1] + [trade(a, 1) for a in waiting]
    paired = [(a.astype(F32) + b.astype(F32)).astype(BF16) for a, b in zip(local, pairs)]
    cuts_of = pair_chunks(rows, border)
    borders = [trade(a[low:high], 2 * i + 2) for i, a in enumerate(paired) for low, high in cuts_of]
    prepared = pl.pallas_call(
        functools.partial(prepare_kernel, cuts, reps, subs),
        out_shape=[
            shape((2 * units, units), BF16),
            shape((1, units), F32),
            shape((1, units), F32),
            shape((border, rows), BF16),
            shape((rows, rows), F32),
            shape((rows, rows), BF16),
            shape((rows, rows), BF16),
        ],
        in_specs=[pl.BlockSpec(memory_space=pl.ANY)] + [hbm] * 9,
        out_specs=[vmem] * 7,
        scratch_shapes=[
            *counts_held[1:],
            pltpu.VMEM(degree.shape, jnp.int32),
            pltpu.VMEM(edge_weight.shape[2:], BF16),
            pltpu.VMEM(node_id.shape, jnp.int32),
            pltpu.SemaphoreType.DMA((9,)),
        ],
        compiler_params=pltpu.CompilerParams(vmem_limit_bytes=24 << 20),
        cost_estimate=pl.CostEstimate(flops=WEIGHT, bytes_accessed=4 * units * units, transcendentals=0),
        name="prepare",
    )(
        owns[0] if far else sent[-1],
        *in_hbm(neighbor_count, bcounts, w_self2, w_neigh2, bias1.reshape(1, units), bias2.reshape(1, units)),
        *in_hbm(degree, edge_weight, node_id),
    )
    arrived = slabs + owns + borders
    payload = pl.pallas_call(
        functools.partial(second_layer_kernel, cuts),
        out_shape=shape((rows, units + rows), BF16),
        in_specs=[vmem] * (len(arrived) + 7),
        out_specs=vmem,
        compiler_params=pltpu.CompilerParams(vmem_limit_bytes=24 << 20),
        name="second_layer",
    )(*arrived, *prepared)
    peers = cuts * reps
    moved = lax.all_to_all(
        payload.reshape(peers, rows // peers, units + rows), ("cuts", "rep"), split_axis=0, concat_axis=0, tiled=True
    )
    return pl.pallas_call(
        placing_kernel,
        out_shape=shape((rows, units), BF16),
        in_specs=[vmem],
        out_specs=vmem,
        name="placing",
    )(pltpu.with_memory_space_constraint(moved.reshape(rows, units + rows), pltpu.VMEM))


def solution(mesh):
    block = ("groups", "rep", "sub")
    placed = (
        P(block, "cuts"),
        P("cuts", None),
        P("cuts", None),
        P(),
        P(),
        P(),
        P(),
        P(block, None),
        P(block, None, None),
        P(block, None),
        P(block, None, None, None),
        P(block, None, None),
        P(block, None, None, None, None),
        P(block, "cuts"),
    )
    return jax.shard_map(
        body,
        mesh=mesh,
        in_specs=placed,
        out_specs=P(("groups", "cuts", "rep", "sub"), None),
        check_vma=False,
    )
```

```python
import functools

import jax
import jax.numpy as jnp
from jax import lax
from jax.experimental import pallas as pl
from jax.experimental.pallas import tpu as pltpu
from jax.sharding import PartitionSpec as P

F32 = jnp.float32
BF16 = jnp.bfloat16
VMEM = pltpu.VMEM
SMEM = pltpu.SMEM
DIRECT = 64
WEIGHT = 3_000_000_000


def direct_rows(rows):
    return rows * DIRECT // 128


def pair_chunks(rows, border):
    direct = direct_rows(rows)
    units = (rows - direct + border) // 16
    pieces = 1
    ends = [16 * (units * i // pieces) for i in range(pieces + 1)]
    return list(zip(ends[:-1], ends[1:]))


def partner_pairs(step, total):
    return [(i, i ^ step) for i in range(total)]


def as_column(row):
    n = row.shape[1]
    eye = lax.broadcasted_iota(jnp.int32, (n, n), 0) == lax.broadcasted_iota(jnp.int32, (n, n), 1)
    return jnp.sum(jnp.where(eye, jnp.broadcast_to(row, (n, n)), 0.0), axis=1, keepdims=True)


def live_limit(count_ref, bcount_ref, owner, k):
    return jnp.where(k < count_ref[0, owner], bcount_ref[k, 0, owner], 0)


def live_tile(tile, count_ref, bcount_ref, owner):
    neigh, cap, rows = tile.shape
    slot = lax.broadcasted_iota(jnp.int32, (cap, rows), 0)
    tiles = []
    for k in range(neigh):
        live = slot < live_limit(count_ref, bcount_ref, owner, k)
        tiles.append(jnp.where(live, tile[k].astype(F32), 0.0).astype(BF16))
    return jnp.concatenate(tiles, axis=0)


def contract_first(a, b):
    return lax.dot_general(a, b, (((0,), (0,)), ((), ())), preferred_element_type=F32)


def contract_last(a, b):
    return lax.dot_general(a, b, (((1,), (1,)), ((), ())), preferred_element_type=F32)


def in_hbm(*arrays):
    return [pltpu.with_memory_space_constraint(a, pltpu.HBM) for a in arrays]


def start_all(pairs, sems):
    copies = [pltpu.make_async_copy(src, dst, sems.at[i]) for i, (src, dst) in enumerate(pairs)]
    for copy in copies:
        copy.start()
    return copies


def first_layer_kernel(
    cuts, owners_hbm, count_hbm, bcount_hbm, x_hbm, wn_hbm, ws_hbm, deg_hbm, brow_hbm, ew_hbm, *rest
):
    near, far = min(2, cuts), cuts - min(2, cuts)
    border_refs, own_refs, slab_refs, local_refs = (
        rest[: far // 2],
        rest[far // 2 : far // 2 + far],
        rest[far // 2 + far : far // 2 + far + near],
        rest[far // 2 + far + near : 2 * far + near],
    )
    rest = rest[2 * far + near :]
    owners_ref, count_ref, bcount_ref, brow_v, deg_v, x_v, wn_v, ws_v, ew_v, pick_v, adj_v, *rest = rest
    scale_v, y_v, sums_v, border_v, sems = rest
    pairs = (
        (brow_hbm, brow_v),
        (owners_hbm, owners_ref),
        (count_hbm, count_ref),
        (bcount_hbm, bcount_ref),
        (deg_hbm, deg_v),
        (ew_hbm, ew_v),
        (x_hbm, x_v),
        (wn_hbm, wn_v),
        (ws_hbm, ws_v),
    )
    brow_in, owners_in, *counts_in, deg_in, ew_in, x_in, wn_in, ws_in = start_all(pairs, sems)
    _, _, neigh, cap, rows = ew_v.shape
    total = cuts * rows
    me = lax.axis_index("cuts")
    lane = lax.broadcasted_iota(jnp.int32, (cap, total), 1)
    eye = (
        lax.broadcasted_iota(jnp.int32, (cap, cap), 0) == lax.broadcasted_iota(jnp.int32, (cap, cap), 1)
    ).astype(F32)
    span = min(cuts, 4)

    def fill_picks(first):
        for k in range(neigh):
            columns = contract_last(eye, brow_v[0, k].astype(F32)).astype(jnp.int32)
            for u in range(span):
                target = columns[:, first + u : first + u + 1] + owners_ref[k, 0, first + u] * rows
                at = u * neigh * cap + k * cap
                pick_v[at : at + cap, :] = (lane == target).astype(F32).astype(BF16)

    brow_in.wait()
    owners_in.wait()
    for first in range(0, cuts, span):
        fill_picks(first)
        if first == 0:
            for copy in (*counts_in, deg_in, ew_in):
                copy.wait()
        for u in range(first, first + span):
            at = slice(u * rows, (u + 1) * rows)
            picks = pick_v[(u - first) * neigh * cap : (u - first + 1) * neigh * cap, :]
            adj_v[at, :] = contract_first(live_tile(ew_v[0, u], count_ref, bcount_ref, u), picks).astype(BF16)
            scale_v[at, :] = as_column(1.0 / deg_v[:, at].astype(F32))
    x_in.wait()
    wn_in.wait()
    for first in range(0, cuts, span):
        at = slice(first * rows, (first + span) * rows)
        y_v[at, :] = jnp.dot(x_v[at, :], wn_v[...], preferred_element_type=F32).astype(BF16)
    ws_in.wait()
    for first in range(0, cuts, span):
        at = slice(first * rows, (first + span) * rows)
        selfs = jnp.dot(x_v[at, :], ws_v[...], preferred_element_type=F32)
        summed = jnp.dot(adj_v[at, :], y_v[...], preferred_element_type=F32)
        sums_v[at, :] = (selfs + summed * scale_v[at, :]).astype(BF16)
    for first in range(0, cuts, span):
        if span < cuts:
            fill_picks(first)
        at = slice(first * neigh * cap, (first + span) * neigh * cap)
        border_v[at, :] = jnp.dot(pick_v[...], sums_v[...], preferred_element_type=F32).astype(BF16)
    direct = direct_rows(rows)
    border = neigh * cap

    def own_at(owner, first, size):
        return pl.ds(pl.multiple_of(owner * rows + first, 16), size)

    def paired_part(out_ref, owner):
        out_ref[: rows - direct, :] = sums_v[own_at(owner, direct, rows - direct), :]
        out_ref[rows - direct :, :] = border_v[pl.ds(pl.multiple_of(owner * border, border), border), :]

    for i, out_ref in enumerate(border_refs):
        paired_part(out_ref, me ^ (2 * i + 3))
    for i, out_ref in enumerate(own_refs):
        out_ref[...] = sums_v[own_at(me ^ (i + 2), 0, direct), :]
    for step, out_ref in enumerate(slab_refs):
        out_ref[:direct, :] = sums_v[own_at(me ^ step, 0, direct), :]
        paired_part(out_ref.at[pl.ds(direct, rows - direct + border)], me ^ step)
    for i, out_ref in enumerate(local_refs):
        paired_part(out_ref, me ^ (2 * i + 2))


def hidden_rows(parts, b1_ref):
    total = parts[0].astype(F32)
    for part in parts[1:]:
        total = total + part.astype(F32)
    return jnp.maximum(total + b1_ref[...], 0.0).astype(BF16)


def prepare_kernel(cuts, reps, subs, after_ref, *rest):
    count_hbm, bcount_hbm, ws_hbm, wn_hbm, b1_hbm, b2_hbm, deg_hbm, ew_hbm, id_hbm = rest[:9]
    w_ref, b1_ref, b2_ref, live_ref, scale_ref, chosen_ref, slots_ref = rest[9:16]
    count_ref, bcount_ref, deg_v, ew_v, id_v, sems = rest[16:]
    units = ws_hbm.shape[0]
    rows = ew_v.shape[2]
    me = lax.axis_index("cuts")
    pairs = (
        (count_hbm, count_ref),
        (bcount_hbm, bcount_ref),
        (deg_hbm, deg_v),
        (id_hbm, id_v),
        (ew_hbm.at[0, me], ew_v),
        (b1_hbm, b1_ref),
        (b2_hbm, b2_ref),
        (ws_hbm, w_ref.at[pl.ds(0, units)]),
        (wn_hbm, w_ref.at[pl.ds(units, units)]),
    )
    copies = start_all(pairs, sems)
    for copy in copies[:5]:
        copy.wait()
    live_ref[...] = live_tile(ew_v[...], count_ref, bcount_ref, me)
    degrees = deg_v[:, pl.ds(pl.multiple_of(me * rows, rows), rows)].astype(F32)
    scale_ref[...] = jnp.broadcast_to(as_column(1.0 / degrees), (rows, rows))
    ids = id_v[...]
    device = ids // rows
    peer = (device // (reps * subs)) * reps + (device // subs) % reps
    slot = (ids - device * rows).astype(F32)
    peer_f = peer.astype(F32)
    down = lax.broadcasted_iota(jnp.int32, (rows, rows), 0)
    across = lax.broadcasted_iota(jnp.int32, (rows, rows), 1)
    earlier = (as_column(peer_f) == peer_f) & (down < across)
    rank = jnp.sum(earlier.astype(F32), axis=0, keepdims=True).astype(jnp.int32)
    place = peer * (rows // (cuts * reps)) + rank
    chosen = down == place
    chosen_ref[...] = chosen.astype(F32).astype(BF16)
    slots = jnp.sum(jnp.where(chosen, slot, 0.0), axis=1, keepdims=True)
    slots_ref[...] = jnp.broadcast_to(slots, (rows, rows)).astype(BF16)
    for copy in copies[5:]:
        copy.wait()


def second_layer_kernel(cuts, *rest):
    near, far = min(2, cuts), cuts - min(2, cuts)
    slab_refs, own_refs, border_refs = rest[:near], rest[near : near + far], rest[near + far : -8]
    w_ref, b1_ref, b2_ref, live_ref, scale_ref, chosen_ref, slots_ref, out_ref = rest[-8:]
    rows = chosen_ref.shape[0]
    chunks = pair_chunks(rows, live_ref.shape[0])
    units = w_ref.shape[1]
    direct = direct_rows(rows)
    first = hidden_rows([slab[:direct, :] for slab in slab_refs] + [part[...] for part in own_refs], b1_ref)
    pieces = []
    for i, (low, high) in enumerate(chunks):
        parts = [slab[direct + low : direct + high, :] for slab in slab_refs]
        pieces.append(hidden_rows(parts + [part[...] for part in border_refs[i :: len(chunks)]], b1_ref))
    others = jnp.concatenate(pieces, axis=0)
    own = jnp.concatenate([first, others[: rows - direct]], axis=0)
    border = others[rows - direct :]
    summed = contract_first(live_ref[...], border)
    mean = (summed * scale_ref[:, :1]).astype(BF16)
    z = jnp.dot(jnp.concatenate([own, mean], axis=1), w_ref[...], preferred_element_type=F32) + b2_ref[...]
    scale = lax.rsqrt(jnp.mean(z * z, axis=1, keepdims=True) + 1e-05)
    normalized = (z * scale).astype(BF16)
    out_ref[:, :units] = jnp.dot(chosen_ref[...], normalized, preferred_element_type=F32).astype(BF16)
    out_ref[:, units:] = slots_ref[...]


def placing_kernel(in_ref, out_ref):
    rows, units = out_ref.shape
    across = lax.broadcasted_iota(jnp.int32, (rows, rows), 1)
    chosen = in_ref[:, units:].astype(F32).astype(jnp.int32) == across
    out_ref[...] = contract_first(chosen.astype(F32).astype(BF16), in_ref[:, :units]).astype(BF16)


def body(
    features,
    w_self1,
    w_neigh1,
    bias1,
    w_self2,
    w_neigh2,
    bias2,
    degree,
    neighbor_owners,
    neighbor_count,
    boundary_rows,
    boundary_count,
    edge_weight,
    node_id,
):
    cuts, reps, subs = (lax.axis_size(a) for a in ("cuts", "rep", "sub"))
    total, width = features.shape
    units = w_self1.shape[1]
    _, _, neigh, cap, rows = edge_weight.shape
    border = neigh * cap
    vmem = pl.BlockSpec(memory_space=VMEM)
    hbm = pl.BlockSpec(memory_space=pltpu.HBM)
    shape = jax.ShapeDtypeStruct
    slab = shape((rows + border, units), BF16)
    direct = direct_rows(rows)
    own_slab, border_slab = shape((direct, units), BF16), shape((rows - direct + border, units), BF16)
    near, far = min(2, cuts), cuts - min(2, cuts)
    owners = neighbor_owners.transpose(2, 0, 1)
    bcounts = boundary_count.transpose(2, 0, 1)
    brows = boundary_rows.transpose(0, 2, 1, 3)
    counts_held = [SMEM(a.shape, jnp.int32) for a in (owners, neighbor_count, bcounts)]
    held = total * width + 2 * width * units + total * total + 2 * total * units + 256 * total
    held += min(cuts, 4) * border * total + cuts * border * (units + rows) + units * (near * (rows + border) + far * (rows + border))
    sent = pl.pallas_call(
        functools.partial(first_layer_kernel, cuts),
        out_shape=[border_slab] * (far // 2)
        + [own_slab] * far
        + [slab] * near
        + [border_slab] * (far // 2),
        in_specs=[hbm] * 9,
        out_specs=[vmem] * (2 * far + near),
        scratch_shapes=[
            *counts_held,
            pltpu.VMEM(brows.shape, jnp.int32),
            pltpu.VMEM(degree.shape, jnp.int32),
            pltpu.VMEM((total, width), BF16),
            pltpu.VMEM((width, units), BF16),
            pltpu.VMEM((width, units), BF16),
            pltpu.VMEM(edge_weight.shape, BF16),
            pltpu.VMEM((min(cuts, 4) * border, total), BF16),
            pltpu.VMEM((total, total), BF16),
            pltpu.VMEM((total, 1), F32),
            pltpu.VMEM((total, units), BF16),
            pltpu.VMEM((total, units), BF16),
            pltpu.VMEM((cuts * border, units), BF16),
            pltpu.SemaphoreType.DMA((9,)),
        ],
        compiler_params=pltpu.CompilerParams(vmem_limit_bytes=2 * held + (8 << 20)),
        name="first_layer",
    )(*in_hbm(owners, neighbor_count, bcounts, features, w_neigh1, w_self1, degree, brows, edge_weight))
    sent = list(sent)
    pairs, owns, slabs, local = (
        sent[: far // 2],
        sent[far // 2 : far // 2 + far],
        sent[far // 2 + far : far // 2 + far + near],
        sent[far // 2 + far + near :],
    )
    trade = lambda a, step: lax.ppermute(a, "cuts", partner_pairs(step, cuts))
    pairs = [trade(a, 1) for a in pairs]
    owns = [trade(a, i + 2) for i, a in enumerate(owns)]
    pairs, waiting = lax.optimization_barrier((pairs, slabs[1:]))
    slabs = slabs[:1] + [trade(a, 1) for a in waiting]
    paired = [(a.astype(F32) + b.astype(F32)).astype(BF16) for a, b in zip(local, pairs)]
    cuts_of = pair_chunks(rows, border)
    borders = [trade(a[low:high], 2 * i + 2) for i, a in enumerate(paired) for low, high in cuts_of]
    prepared = pl.pallas_call(
        functools.partial(prepare_kernel, cuts, reps, subs),
        out_shape=[
            shape((2 * units, units), BF16),
            shape((1, units), F32),
            shape((1, units), F32),
            shape((border, rows), BF16),
            shape((rows, rows), F32),
            shape((rows, rows), BF16),
            shape((rows, rows), BF16),
        ],
        in_specs=[pl.BlockSpec(memory_space=pl.ANY)] + [hbm] * 9,
        out_specs=[vmem] * 7,
        scratch_shapes=[
            *counts_held[1:],
            pltpu.VMEM(degree.shape, jnp.int32),
            pltpu.VMEM(edge_weight.shape[2:], BF16),
            pltpu.VMEM(node_id.shape, jnp.int32),
            pltpu.SemaphoreType.DMA((9,)),
        ],
        compiler_params=pltpu.CompilerParams(vmem_limit_bytes=24 << 20),
        cost_estimate=pl.CostEstimate(flops=WEIGHT, bytes_accessed=4 * units * units, transcendentals=0),
        name="prepare",
    )(
        owns[1] if far else sent[-1],
        *in_hbm(neighbor_count, bcounts, w_self2, w_neigh2, bias1.reshape(1, units), bias2.reshape(1, units)),
        *in_hbm(degree, edge_weight, node_id),
    )
    arrived = slabs + owns + borders
    payload = pl.pallas_call(
        functools.partial(second_layer_kernel, cuts),
        out_shape=shape((rows, units + rows), BF16),
        in_specs=[vmem] * (len(arrived) + 7),
        out_specs=vmem,
        compiler_params=pltpu.CompilerParams(vmem_limit_bytes=24 << 20),
        name="second_layer",
    )(*arrived, *prepared)
    peers = cuts * reps
    moved = lax.all_to_all(
        payload.reshape(peers, rows // peers, units + rows), ("cuts", "rep"), split_axis=0, concat_axis=0, tiled=True
    )
    return pl.pallas_call(
        placing_kernel,
        out_shape=shape((rows, units), BF16),
        in_specs=[vmem],
        out_specs=vmem,
        name="placing",
    )(pltpu.with_memory_space_constraint(moved.reshape(rows, units + rows), pltpu.VMEM))


def solution(mesh):
    block = ("groups", "rep", "sub")
    placed = (
        P(block, "cuts"),
        P("cuts", None),
        P("cuts", None),
        P(),
        P(),
        P(),
        P(),
        P(block, None),
        P(block, None, None),
        P(block, None),
        P(block, None, None, None),
        P(block, None, None),
        P(block, None, None, None, None),
        P(block, "cuts"),
    )
    return jax.shard_map(
        body,
        mesh=mesh,
        in_specs=placed,
        out_specs=P(("groups", "cuts", "rep", "sub"), None),
        check_vma=False,
    )
```
